256 devices in a mesh: group: 8 (over z), sub: 32 (over x, y, core).
Axes of the slice: x: 4, y: 4, z: 8, core: 2. Of those that a mesh axis runs over, the one named last changes fastest.
Arguments:
- right_sides: float32 [6, 512, 32, 128], P(None, ('group', 'sub')), may hold values from -6 to 6
- lower_inv: bfloat16 [6, 512, 128, 128], P(None, ('group', 'sub'))
- upper_inv: bfloat16 [6, 512, 128, 128], P(None, ('group', 'sub'))
- lower_off: bfloat16 [15, 512, 4, 128, 128], P(None, ('group', 'sub')), may hold values from -0.125 to 0.125
- upper_off: bfloat16 [15, 512, 4, 128, 128], P(None, ('group', 'sub')), may hold values from -0.125 to 0.125
- lower_pattern: int32 [15, 512, 4], P(None, ('group', 'sub')), may hold values from 0 to 255, as said below
- upper_pattern: int32 [15, 512, 4], P(None, ('group', 'sub')), may hold values from 0 to 255, as said below
Outputs:
- solution: float32 [6, 512, 32, 128], P(None, ('group', 'sub'))
The draws below stay inside these ranges and needn't reach their ends.
Inputs may be any that keep to these rules, and one draw needn't show every extreme that they name: `lower_pattern`: entry [p, i, n], for the pair p = k (k - 1) / 2 + l of a level l and a deeper level k, is below 512 // 2^k. `upper_pattern`: entry [p, i, n], for the pair p = k (k - 1) / 2 + l of a level l and a deeper level k, is below 512 // 2^k.
All inputs are finite; a program needn't handle non-finite values.
Results may differ from the reference program's by a relative error of at most 0.017.
Values may be sent and summed in bfloat16 or wider, within the bound.
No kernel may reach another device: no remote copies, remote signals or barrier semaphores. Data moves between devices by JAX's collectives and lax.ppermute only.
A program may use at most 64 MiB of HBM per device.

```python
import math
import jax
import jax.numpy as jnp
import numpy as np
from jax import lax

BLK = 128
NRHS = 32
LEVELS = 6
NNZ = 4
PAIRS = 15
NBLK = 512


def inverse_blocks(key, diag_low, diag_high, noise_scale):
    diag_key, noise_key = jax.random.split(key)
    diag_part = jax.random.uniform(diag_key, (LEVELS, NBLK, BLK), jnp.float32, diag_low, diag_high)
    off_part = jax.random.normal(noise_key, (LEVELS, NBLK, BLK, BLK), jnp.float32) * (noise_scale / math.sqrt(BLK))
    identity = jnp.eye(BLK, dtype=jnp.float32)
    return (off_part + identity * diag_part[..., :, None]).astype(jnp.bfloat16)


def pattern_table(key):
    entry_key, pick_key = jax.random.split(key)
    spans = np.array([NBLK // 2 ** deeper for deeper in range(1, LEVELS) for shallow in range(deeper)], dtype=np.int32)
    span_table = jnp.asarray(spans)[:, None, None]
    values = jax.random.randint(entry_key, (PAIRS, NBLK, NNZ), 0, span_table, dtype=jnp.int32)
    chosen = jax.random.randint(pick_key, (), 0, NBLK, dtype=jnp.int32)
    return values.at[0, chosen, 0].set(NBLK // 2 - 1)


def draw_lower_inv(key, part):
    key = jax.random.fold_in(key, 11)
    return inverse_blocks(key, 0.8, 1.2, 0.5)


def draw_upper_inv(key, part):
    key = jax.random.fold_in(key, 12)
    return inverse_blocks(key, 0.8, 1.2, 0.5)


def draw_lower_pattern(key, part):
    key = jax.random.fold_in(key, 21)
    return pattern_table(key)


def draw_upper_pattern(key, part):
    key = jax.random.fold_in(key, 22)
    return pattern_table(key)


def steps_of(own_key, extent, cuts, low, high):
    level, own = 1.0, jax.random.fold_in(own_key, 6)
    for position, parts in cuts:
        heights = jnp.exp(jax.random.uniform(jax.random.fold_in(own, position), (parts,), jnp.float32, low / len(cuts), high / len(cuts)))
        level = level * jnp.repeat(heights, extent[position] // parts).reshape([-1 if axis == position else 1 for axis in range(len(extent))])
    return level


def bell_draw(rng, shape, scale, bound, cuts=(), held_as=jnp.bfloat16):
    drawn = jax.random.normal(rng, shape, jnp.float32) * scale
    if len(cuts) > 0:
        drawn = steps_of(rng, shape, cuts, -0.22, 0.18) * drawn
    return jnp.clip(drawn, min=-bound, max=bound).astype(held_as)


def setup_inputs(seed: int = 0) -> dict:
    key_list = jax.random.split(jax.random.key(seed), 8)
    return {
        "right_sides": bell_draw(key_list[0], (LEVELS, NBLK, NRHS, BLK), 1.0, 6.0, ((1, 256),), jnp.float32),
        "lower_inv": draw_lower_inv(jax.random.fold_in(key_list[7], 71), 0),
        "upper_inv": draw_upper_inv(jax.random.fold_in(key_list[7], 71), 0),
        "lower_off": bell_draw(key_list[3], (PAIRS, NBLK, NNZ, BLK, BLK), (BLK * NNZ * (LEVELS - 1)) ** -0.5, 0.125, ((1, 256),)),
        "upper_off": bell_draw(key_list[4], (PAIRS, NBLK, NNZ, BLK, BLK), (BLK * NNZ * (LEVELS - 1)) ** -0.5, 0.125, ((1, 256),)),
        "lower_pattern": draw_lower_pattern(jax.random.fold_in(key_list[7], 71), 0),
        "upper_pattern": draw_upper_pattern(jax.random.fold_in(key_list[7], 71), 0),
    }


def settle(values):
    return lax.optimization_barrier(values.astype(jnp.bfloat16)).astype(jnp.float32)


def apply_inverse(residual, inverse):
    return jnp.einsum("irb,ibc->irc", settle(residual), inverse.astype(jnp.float32), precision=lax.Precision.HIGHEST)


def source_rows(pattern, deeper, pair_index):
    block_ids = jnp.arange(NBLK, dtype=jnp.int32)
    span_rows = NBLK // 2 ** deeper
    return ((block_ids // span_rows) * span_rows)[:, None] + pattern[pair_index].astype(jnp.int32)


def couple(rounded, rows_index, blocks):
    picked = rounded[rows_index]
    return jnp.einsum("inrb,inbc->irc", picked, blocks.astype(jnp.float32), precision=lax.Precision.HIGHEST)


def reference(right_sides, lower_inv, upper_inv, lower_off, upper_off, lower_pattern, upper_pattern):
    pending = [jnp.zeros((NBLK, NRHS, BLK), jnp.float32) for level in range(LEVELS)]
    forward = [None] * LEVELS
    for deeper in range(LEVELS - 1, -1, -1):
        forward[deeper] = apply_inverse(right_sides[deeper] - pending[deeper], lower_inv[deeper])
        rounded = settle(forward[deeper])
        for shallow in range(deeper):
            pair_index = deeper * (deeper - 1) // 2 + shallow
            rows_index = source_rows(lower_pattern, deeper, pair_index)
            pending[shallow] = pending[shallow] + couple(rounded, rows_index, lower_off[pair_index])
    backlog = [jnp.zeros((NBLK, NRHS, BLK), jnp.float32) for level in range(LEVELS)]
    results = [None] * LEVELS
    for shallow in range(LEVELS):
        results[shallow] = apply_inverse(forward[shallow] - backlog[shallow], upper_inv[shallow])
        rounded = settle(results[shallow])
        for deeper in range(shallow + 1, LEVELS):
            pair_index = deeper * (deeper - 1) // 2 + shallow
            rows_index = source_rows(upper_pattern, deeper, pair_index)
            backlog[deeper] = backlog[deeper] + couple(rounded, rows_index, upper_off[pair_index])
    return jnp.stack(results)
```

```python
import functools

import jax
import jax.numpy as jnp
from jax import lax
from jax.experimental import pallas as pl
from jax.experimental.pallas import tpu as pltpu
from jax.sharding import PartitionSpec as P

SUB_BITS = 5
PLANE = 64
VMEM = pl.BlockSpec(memory_space=pltpu.VMEM)
SMEM = pl.BlockSpec(memory_space=pltpu.SMEM)
PARAMS = pltpu.CompilerParams(vmem_limit_bytes=20 * 2**20)


def pair(deeper, shallow):
    return deeper * (deeper - 1) // 2 + shallow


def span(masks):
    groups, seen = [], set()
    for first in range(1 << SUB_BITS):
        if first not in seen:
            group = [first]
            for mask in masks:
                group = group + [member ^ mask for member in group]
            seen.update(group)
            groups.append(sorted(group))
    return groups


def swapped(block, axis, mask):
    return lax.ppermute(block, axis, [(i, i ^ mask) for i in range(lax.axis_size(axis))])


def spread(block, masks):
    ways = 1 << len(masks)
    copies = jnp.broadcast_to(block[None], (ways,) + block.shape).reshape((-1,) + block.shape[1:])
    return lax.all_to_all(copies, "sub", 0, 0, tiled=True, axis_index_groups=span(masks))


def collected(block, masks):
    own = spread(block, masks)
    return own, swapped(own, "sub", 1)


def place(local, core):
    index = (local >> 2 << 1) | (local & 1)
    other = (local >> 1 & 1) ^ core
    return index | other << 8


def read(kind, refs, code, slot):
    index = code & 255
    if kind == "one":
        return refs[0][index]
    if kind == "planes":
        return refs[0][(code >> 9) * 8 + slot]
    near = jnp.where((code >> 8 & 1) == 0, refs[0][index], refs[1][index])
    if kind == "halves":
        return near
    return jnp.where(code >> 9 == 0, near, refs[2][slot])


def update_kernel(plan, first, level, inverses, outs, *refs):
    refs = list(refs)
    base = refs.pop(0)
    codes, off = (refs.pop(0), refs.pop(0)) if plan else (None, None)
    near = []
    for kind, _ in plan:
        count = {"one": 1, "planes": 1, "halves": 2, "far": 3}[kind]
        near.append([refs.pop(0) for _ in range(count)])
    inverse = [refs.pop(0) for _ in range(inverses)]
    for j in range(2):
        total = base[first, j] if first is not None else base[j]
        for (kind, p), buffers in zip(plan, near):
            picked = [read(kind, buffers, codes[p, j * 4 + n], j * 4 + n) for n in range(4)]
            total = total - jnp.dot(
                jnp.concatenate(picked, 1),
                off[p, j].reshape(512, 128),
                preferred_element_type=jnp.float32,
            )
        at = 0
        if not inverses:
            refs[at][j] = total
            at += 1
        for matrix in inverse:
            total = jnp.dot(
                total.astype(jnp.bfloat16), matrix[level, j], preferred_element_type=jnp.float32
            )
            refs[at][j] = total
            at += 1
        if outs > at:
            refs[at][j] = total.astype(jnp.bfloat16)


def update(base, first, plan, near, codes, off, level=0, inverse=(), low=False):
    block = (2,) + base.shape[-2:]
    shapes = [jax.ShapeDtypeStruct(block, jnp.float32)] * max(1, len(inverse))
    shapes += [jax.ShapeDtypeStruct(block, jnp.bfloat16)] * low
    arguments = [base] + ([codes, off] if plan else [])
    for buffers in near:
        arguments += list(buffers)
    arguments += list(inverse)
    specs = [SMEM if argument is codes and plan else VMEM for argument in arguments]
    products = 2 * (4 * len(plan) + len(inverse))
    return pl.pallas_call(
        functools.partial(update_kernel, tuple(plan), first, level, len(inverse), len(shapes)),
        out_shape=shapes,
        in_specs=specs,
        out_specs=[VMEM] * len(shapes),
        compiler_params=PARAMS,
        cost_estimate=pl.CostEstimate(
            flops=products * 2 * 32 * 128 * 128, bytes_accessed=products * 32768, transcendentals=0
        ),
    )(*arguments)


def pick_kernel(kind, codes, *refs):
    out = refs[-1]
    for slot in range(out.shape[0]):
        out[slot] = read(kind, refs[:-1], codes[slot // 8, slot % 8], slot)


def pick(codes, buffers):
    count = codes.shape[0] * 8
    block = buffers[0].shape[1:]
    return pl.pallas_call(
        functools.partial(pick_kernel, "halves"),
        out_shape=jax.ShapeDtypeStruct((count,) + block, jnp.bfloat16),
        in_specs=[SMEM] + [VMEM] * len(buffers),
        out_specs=VMEM,
        compiler_params=PARAMS,
        cost_estimate=pl.CostEstimate(flops=0, bytes_accessed=count * 16384, transcendentals=0),
    )(codes, *buffers)


def on_device(
    right_sides, lower_inv, upper_inv, lower_off, upper_off, lower_pattern, upper_pattern
):
    sub, group = lax.axis_index("sub"), lax.axis_index("group")
    core = sub & 1
    half = [[0, 1, 2, 3], [4, 5, 6, 7]]

    lower_pattern, upper_pattern = (x.reshape(-1, 8) for x in (lower_pattern, upper_pattern))
    asked = jnp.stack([lower_pattern[:3], upper_pattern[:3]])
    beside = swapped(asked, "group", 1)
    both = jnp.stack([asked[:, 0], beside[:, 0]])
    every = jnp.concatenate([both, swapped(both, "group", 2)])
    every = every[jnp.arange(4) ^ (group & 3)]
    beside = place(beside % PLANE, core)
    every = place(every % PLANE, core)

    low_code, up_code = [], []
    for deeper in range(1, 6):
        for shallow in range(deeper):
            value, wanted = lower_pattern[pair(deeper, shallow)], upper_pattern[pair(deeper, shallow)]
            if deeper == 5:
                low_code.append(value)
            else:
                plane = value // PLANE
                plane = plane ^ (group & 1) if deeper == 2 else plane
                low_code.append(place(value % PLANE, core) | plane << 9)
            if shallow == 4:
                up_code.append(wanted)
            else:
                plane = wanted // PLANE
                plane = plane ^ (group & 1) if deeper == 2 else plane
                local = wanted % PLANE
                if deeper == 4 and shallow < 3:
                    local = local + (sub >> 4) * 32
                if deeper == 5:
                    local = local + ((sub >> 3) & (3 if shallow < 3 else 1)) * 16
                up_code.append(place(local, core) | plane << 9)
    low_code, up_code = jnp.stack(low_code), jnp.stack(up_code)

    low = functools.partial(update, codes=low_code, off=lower_off)
    up = functools.partial(update, codes=up_code, off=upper_off)

    row, square, plane = (2, 4), (2, 4, 8), (2, 4, 8, 16)
    f5, sent = low(right_sides, 5, [], [], level=5, inverse=[lower_inv], low=True)
    near5 = [spread(sent, (1, 2, 4))]
    f4, sent = low(right_sides, 4, [("one", 14)], [near5], level=4, inverse=[lower_inv], low=True)
    near4 = collected(sent, square)
    (r3,) = low(right_sides, 3, [("one", 13)], [near5])
    f3, sent = low(r3, None, [("halves", 9)], [near4], level=3, inverse=[lower_inv], low=True)
    near3 = collected(sent, plane)
    (r2,) = low(right_sides, 2, [("one", 12), ("halves", 8)], [near5, near4])
    f2, sent = low(r2, None, [("halves", 5)], [near3], level=2, inverse=[lower_inv], low=True)
    near2 = collected(sent, plane)
    (r1,) = low(right_sides, 1, [("one", 11), ("halves", 7), ("halves", 4)], [near5, near4, near3])
    far2 = swapped(pick(beside[0, 2:3], near2), "group", 1)
    more2 = swapped(pick(beside[0, 1:2], near2), "group", 1)
    f1, sent = low(
        r1, None, [("far", 2)], [near2 + (far2,)], level=1, inverse=[lower_inv], low=True
    )
    near1 = collected(sent, plane)
    (r0,) = low(
        right_sides,
        0,
        [("one", 10), ("halves", 6), ("halves", 3), ("far", 1)],
        [near5, near4, near3, near2 + (more2,)],
    )
    asked1 = lax.all_to_all(
        pick(every[:, 0], near1), "group", 0, 0, tiled=True, axis_index_groups=half
    )
    _, s0, sent = low(
        r0, None, [("planes", 0)], [[asked1]], level=0, inverse=[lower_inv, upper_inv], low=True
    )

    near0 = collected(sent, plane)
    asked0 = lax.all_to_all(
        pick(every[:, 1], near0), "group", 0, 0, tiled=True, axis_index_groups=half
    )
    more0 = swapped(pick(beside[1, 1:2], near0), "group", 1)
    s1, sent = up(f1, None, [("planes", 0)], [[asked0]], level=1, inverse=[upper_inv], low=True)
    near1 = collected(sent, plane)
    (r2,) = up(f2, None, [("far", 1)], [near0 + (more0,)])
    far1 = swapped(pick(beside[1, 2:3], near1), "group", 1)
    s2, sent = up(
        r2, None, [("far", 2)], [near1 + (far1,)], level=2, inverse=[upper_inv], low=True
    )
    near2 = collected(sent, plane)
    (r3,) = up(f3, None, [("halves", 3), ("halves", 4)], [near0, near1])
    s3, sent = up(r3, None, [("halves", 5)], [near2], level=3, inverse=[upper_inv], low=True)
    near3 = collected(sent, square)
    (r4,) = up(f4, None, [("halves", 6), ("halves", 7), ("halves", 8)], [near0, near1, near2])
    s4, sent = up(r4, None, [("halves", 9)], [near3], level=4, inverse=[upper_inv], low=True)
    near4 = [spread(sent, (1, 2, 4))]
    (r5,) = up(
        f5,
        None,
        [("halves", 10), ("halves", 11), ("halves", 12), ("halves", 13)],
        [near0, near1, near2, near3],
    )
    (s5,) = up(r5, None, [("one", 14)], [near4], level=5, inverse=[upper_inv])
    return jnp.stack([s0, s1, s2, s3, s4, s5])


def solution(mesh):
    return jax.shard_map(
        on_device,
        mesh=mesh,
        in_specs=(
            P(None, ("group", "sub"), None, None),
            P(None, ("group", "sub"), None, None),
            P(None, ("group", "sub"), None, None),
            P(None, ("group", "sub"), None, None, None),
            P(None, ("group", "sub"), None, None, None),
            P(None, ("group", "sub"), None),
            P(None, ("group", "sub"), None),
        ),
        out_specs=P(None, ("group", "sub"), None, None),
        check_vma=False,
    )
```

```python
import functools

import jax
import jax.numpy as jnp
from jax import lax
from jax.experimental import pallas as pl
from jax.experimental.pallas import tpu as pltpu
from jax.sharding import PartitionSpec as P

SUB_BITS = 5
PLANE_BITS = 6
PLANE = 1 << PLANE_BITS
VMEM = pl.BlockSpec(memory_space=pltpu.VMEM)
SMEM = pl.BlockSpec(memory_space=pltpu.SMEM)
HBM = pl.BlockSpec(memory_space=pl.ANY)
PARAMS = pltpu.CompilerParams(vmem_limit_bytes=8 * 2**20)


def span(masks):
    groups, seen = [], set()
    for first in range(1 << SUB_BITS):
        if first not in seen:
            group = [first]
            for mask in masks:
                group = group + [member ^ mask for member in group]
            seen.update(group)
            groups.append(sorted(group))
    return groups


def swapped(block, axis, mask):
    return lax.ppermute(block, axis, [(i, i ^ mask) for i in range(lax.axis_size(axis))])


def spread(copies, masks):
    return lax.all_to_all(copies, "sub", 0, 0, tiled=True, axis_index_groups=span(masks))


def collected(copies, masks):
    own = spread(copies, masks)
    return own, swapped(own, "sub", 1)


def planes(copies):
    half = [[0, 1, 2, 3], [4, 5, 6, 7]]
    return lax.all_to_all(copies, "group", 0, 0, tiled=True, axis_index_groups=half)


def after(value, *others):
    return lax.optimization_barrier((value,) + others)[0]


def in_vmem(value):
    return pltpu.with_memory_space_constraint(value, pltpu.VMEM)


def in_smem(value):
    return pltpu.with_memory_space_constraint(value, pltpu.SMEM)


def in_hbm(value):
    return pltpu.with_memory_space_constraint(value, pltpu.HBM)


CORE, ODD, MINE, START16, START8, START8IN16, NONE = range(7)


def positions(sub, group):
    return jnp.stack(
        [sub & 1, group & 1, group & 3, (sub >> 4) * 32, (sub >> 3) * 16, (sub >> 3 & 1) * 16]
    )


def block(own, other, local, core):
    index = (local >> 2 << 1) | (local & 1)
    return jnp.where((local >> 1 & 1) == core, own[index], other[index])


def read(kind, start, refs, me, wanted, slot):
    if kind == "one":
        return refs[0][wanted]
    if kind == "planes":
        return refs[0][(wanted >> PLANE_BITS) * 8 + slot]
    if kind == "halves":
        local = wanted if start == NONE else wanted + me[start]
        return block(refs[0], refs[1], local, me[CORE])
    near = block(refs[0], refs[1], wanted & PLANE - 1, me[CORE])
    return jnp.where(wanted >> PLANE_BITS == me[ODD], near, refs[2][slot])


def send(ref, j, value):
    value = value.astype(jnp.bfloat16)
    for way in range(ref.shape[0] // 2):
        ref[2 * way + j] = value


FIRST = (14, 13, 9, 12, 8, 5)
BUFFERS = {"one": 1, "planes": 1, "halves": 2, "far": 3}


def coupled(total, j, plan, near, side, me, table, off):
    for (kind, p, start, shift), buffers in zip(plan, near):
        at = FIRST.index(p) if off.shape[0] == len(FIRST) else p
        matrices = off[at, j].reshape(512, 128)
        picked = [
            read(kind, start, buffers, me, table[2 * side + j, n, p], shift + j * 4 + n)
            for n in range(4)
        ]
        total = total - jnp.dot(
            jnp.concatenate(picked, 1), matrices, preferred_element_type=jnp.float32
        )
    return total


def times(total, matrix):
    return jnp.dot(total.astype(jnp.bfloat16), matrix, preferred_element_type=jnp.float32)


def update_kernel(plan, side, first, level, inverses, ways, me, table, off, base, *refs):
    refs = list(refs)
    near = [[refs.pop(0) for _ in range(BUFFERS[entry[0]])] for entry in plan]
    inverse = [refs.pop(0) for _ in range(inverses)]
    for j in range(2):
        total = base[first, j] if first is not None else base[j]
        total = coupled(total, j, plan, near, side, me, table, off)
        if not inverses:
            refs[0][j] = total
        for matrix in inverse:
            total = times(total, matrix[level, j])
        if inverses:
            refs[0][j] = total
        if ways:
            send(refs[-1], j, total)


def update(me, table, off, base, first, plan, near, side, level=0, inverse=(), ways=0):
    shape = (2,) + base.shape[-2:]
    shapes = [jax.ShapeDtypeStruct(shape, jnp.float32)]
    if ways:
        shapes.append(jax.ShapeDtypeStruct((2 * ways,) + shape[1:], jnp.bfloat16))
    arguments = [in_smem(me), in_smem(table), in_vmem(off), in_vmem(base)]
    for buffers in near:
        arguments += list(buffers)
    arguments += [in_vmem(matrix) for matrix in inverse]
    products = 2 * (4 * len(plan) + len(inverse))
    return pl.pallas_call(
        functools.partial(update_kernel, tuple(plan), side, first, level, len(inverse), ways),
        out_shape=shapes,
        in_specs=[SMEM, SMEM] + [VMEM] * (len(arguments) - 2),
        out_specs=[VMEM] * len(shapes),
        compiler_params=PARAMS,
        cost_estimate=pl.CostEstimate(
            flops=products * 2 * 32 * 128 * 128, bytes_accessed=products * 32768, transcendentals=0
        ),
    )(*arguments)


def first_kernel(level, pairs, *refs):
    right, matrix, off, lower, upper = refs[:5]
    out, low, right_kept, matrix_kept, off_kept, table, sems = refs[5:]
    copies = [
        (right, right_kept),
        (matrix, matrix_kept),
        (lower, table.at[pl.ds(0, 2)]),
        (upper, table.at[pl.ds(2, 2)]),
    ]
    copies += [(off.at[p], off_kept.at[at]) for at, p in enumerate(pairs)]
    copies = [pltpu.make_async_copy(*ends, sems.at[at]) for at, ends in enumerate(copies)]
    for copy in copies:
        copy.start()
    copies[0].wait()
    copies[1].wait()
    for j in range(2):
        total = times(right_kept[level, j], matrix_kept[level, j])
        out[j] = total
        send(low, j, total)
    for copy in copies[2:]:
        copy.wait()


def first_update(right_sides, inverse, off, pairs, lower, upper, ways):
    levels = right_sides.shape[0]
    shape = right_sides.shape[1:]
    return pl.pallas_call(
        functools.partial(first_kernel, levels - 1, tuple(pairs)),
        out_shape=[
            jax.ShapeDtypeStruct(shape, jnp.float32),
            jax.ShapeDtypeStruct((2 * ways,) + shape[1:], jnp.bfloat16),
            pltpu.VMEM(right_sides.shape, right_sides.dtype),
            pltpu.VMEM(inverse.shape, inverse.dtype),
            pltpu.VMEM((len(pairs),) + off.shape[1:], off.dtype),
            pltpu.SMEM((4,) + lower.shape[1:], lower.dtype),
        ],
        in_specs=[HBM] * 5,
        out_specs=[VMEM] * 5 + [SMEM],
        scratch_shapes=[pltpu.SemaphoreType.DMA((4 + len(pairs),))],
        compiler_params=PARAMS,
    )(in_hbm(right_sides), in_hbm(inverse), in_hbm(off), in_hbm(lower), in_hbm(upper))


def last_kernel(plan, level, me, table, off, base, *refs):
    refs = list(refs)
    near = [[refs.pop(0) for _ in range(BUFFERS[entry[0]])] for entry in plan]
    inverse = refs.pop(0)
    out, result, sems = refs[-3:]
    copies = [
        pltpu.make_async_copy(ref, out.at[at], sems.at[at]) for at, ref in enumerate(refs[:-3])
    ]
    for copy in copies:
        copy.start()
    for j in range(2):
        total = coupled(base[j], j, plan, near, 1, me, table, off)
        result[j] = times(total, inverse[level, j])
    copies.append(pltpu.make_async_copy(result, out.at[level], sems.at[level]))
    copies[-1].start()
    for copy in copies:
        copy.wait()


def last_update(me, table, off, base, plan, near, inverse, solved):
    levels = len(solved) + 1
    arguments = [in_smem(me), in_smem(table), in_vmem(off), in_vmem(base)]
    for buffers in near:
        arguments += list(buffers)
    arguments += [in_vmem(inverse)] + [in_vmem(value) for value in solved]
    return pl.pallas_call(
        functools.partial(last_kernel, tuple(plan), levels - 1),
        out_shape=jax.ShapeDtypeStruct((levels,) + base.shape, jnp.float32),
        in_specs=[SMEM, SMEM] + [VMEM] * (len(arguments) - 2),
        out_specs=HBM,
        scratch_shapes=[
            pltpu.VMEM(base.shape, jnp.float32),
            pltpu.SemaphoreType.DMA((levels,)),
        ],
        compiler_params=PARAMS,
    )(*arguments)


def stage_kernel(count, *refs):
    sems = refs[-1]
    copies = []
    for at, (ref, kept) in enumerate(zip(refs[:count], refs[count:-1])):
        part = ref.at[pl.ds(0, kept.shape[0])]
        copies.append(pltpu.make_async_copy(part, kept, sems.at[at]))
    for copy in copies:
        copy.start()
    for copy in copies:
        copy.wait()


def staged(space, *arrays, counts=None):
    counts = counts or (None,) * len(arrays)
    shapes = [
        (count or array.shape[0],) + array.shape[1:] for array, count in zip(arrays, counts)
    ]
    return pl.pallas_call(
        functools.partial(stage_kernel, len(arrays)),
        out_shape=[space(shape, array.dtype) for array, shape in zip(arrays, shapes)],
        in_specs=[HBM] * len(arrays),
        out_specs=[VMEM if space is pltpu.VMEM else SMEM] * len(arrays),
        scratch_shapes=[pltpu.SemaphoreType.DMA((len(arrays),))],
        compiler_params=PARAMS,
        cost_estimate=pl.CostEstimate(
            flops=0,
            bytes_accessed=sum(array.size * array.dtype.itemsize for array in arrays),
            transcendentals=0,
        ),
    )(*arrays)


def pick_kernel(plan, side, me, table, *refs):
    out = refs[-1]
    for at, (peer, p, which) in enumerate(plan):
        peer = me[MINE] ^ peer if len(plan) == 4 else peer
        for j in range(2):
            for n in range(4):
                local = table[peer, 2 * side + j, n, p] & PLANE - 1
                out[at * 8 + j * 4 + n] = block(refs[2 * which], refs[2 * which + 1], local, me[CORE])


def pick(me, table, plan, side, *buffers):
    near = [half for pair_of in buffers for half in pair_of]
    shape = near[0].shape[1:]
    return pl.pallas_call(
        functools.partial(pick_kernel, tuple(plan), side),
        out_shape=jax.ShapeDtypeStruct((8 * len(plan),) + shape, jnp.bfloat16),
        in_specs=[SMEM, SMEM] + [VMEM] * len(near),
        out_specs=VMEM,
        compiler_params=PARAMS,
        cost_estimate=pl.CostEstimate(
            flops=0, bytes_accessed=len(plan) * 131072, transcendentals=0
        ),
    )(in_smem(me), in_smem(table), *near)


def halves(p, start=NONE):
    return ("halves", p, start, 0)


def on_device(
    right_sides, lower_inv, upper_inv, lower_off, upper_off, lower_pattern, upper_pattern
):
    sub, group = lax.axis_index("sub"), lax.axis_index("group")
    square, plane = (2, 4, 8), (2, 4, 8, 16)

    tables = [x.transpose(1, 2, 0) for x in (lower_pattern, upper_pattern)]
    mine = jnp.concatenate(tables)
    beside = swapped(mine, "group", 1)

    f5, sent, right, lower_inv, off_first, table = first_update(
        right_sides, lower_inv, lower_off, FIRST, *tables, 8
    )
    (me,) = staged(pltpu.SMEM, after(positions(sub, group), sent))
    near5, beside, me = lax.optimization_barrier((spread(sent, (1, 2, 4)), beside, me))
    near5 = (near5,)
    both = jnp.stack([mine, beside])
    across = swapped(both, "group", 2)
    low_first = functools.partial(update, me, table, off_first, side=0)

    f4, sent = low_first(
        right, 4, [("one", 14, NONE, 0)], [near5], level=4, inverse=[lower_inv], ways=8
    )
    near4 = collected(sent, square)
    (r3,) = low_first(after(right, near4[0]), 3, [("one", 13, NONE, 0)], [near5])
    f3, sent = low_first(r3, None, [halves(9)], [near4], level=3, inverse=[lower_inv], ways=16)
    near3, across = lax.optimization_barrier((spread(sent, plane), across))
    near3 = (near3, swapped(near3, "sub", 1))
    (peers,) = staged(pltpu.SMEM, jnp.concatenate([both, across]))
    (r2,) = low_first(
        after(right, near3[0]), 2, [("one", 12, NONE, 0), halves(8)], [near5, near4]
    )
    near3 = (near3[0], after(near3[1], peers))
    f2, sent = low_first(r2, None, [halves(5)], [near3], level=2, inverse=[lower_inv], ways=16)
    near2 = collected(sent, plane)
    far2 = swapped(pick(me, peers, [(1, 2, 0), (1, 1, 0)], 0, near2), "group", 1)
    lower_off, upper_inv, upper_first = staged(
        pltpu.VMEM,
        in_hbm(after(lower_off, near2[1])),
        in_hbm(after(upper_inv, near2[1])),
        in_hbm(after(upper_off, near2[1])),
        counts=(None, None, 1),
    )
    low = functools.partial(update, me, table, lower_off, side=0)
    (r1,) = low(
        after(right, near2[1]),
        1,
        [("one", 11, NONE, 0), halves(7), halves(4)],
        [near5, near4, near3],
    )
    far2, r1, upper_first = lax.optimization_barrier((far2, r1, upper_first))
    near2 = near2 + (far2,)
    f1, sent = low(
        r1, None, [("far", 2, NONE, 0)], [near2], level=1, inverse=[lower_inv], ways=16
    )
    near1 = collected(sent, plane)
    (r0,) = low(
        after(right, near1[0]),
        0,
        [("one", 10, NONE, 0), halves(6), halves(3), ("far", 1, NONE, 8)],
        [near5, near4, near3, near2],
    )
    near1 = (near1[0], after(near1[1], r0))
    asked = planes(pick(me, peers, [(at, 0, 0) for at in range(4)], 0, near1))
    s0, sent = low(
        r0,
        None,
        [("planes", 0, NONE, 0)],
        [(asked,)],
        level=0,
        inverse=[lower_inv, upper_inv],
        ways=16,
    )

    near0 = collected(sent, plane)
    asked = planes(pick(me, peers, [(at, 0, 0) for at in range(4)], 1, near0))
    s1, sent = update(
        me, table, upper_first, f1, None, [("planes", 0, NONE, 0)], [(asked,)], 1, 1, [upper_inv], 16
    )
    near1 = collected(sent, plane)
    far = swapped(pick(me, peers, [(1, 1, 0), (1, 2, 1)], 1, near0, near1), "group", 1)
    (upper_off,) = staged(pltpu.VMEM, in_hbm(after(upper_off, near1[1])))
    up = functools.partial(update, me, table, upper_off, side=1)
    (r3,) = up(after(f3, near1[1]), None, [halves(3), halves(4)], [near0, near1])
    (r4,) = up(after(f4, near1[1]), None, [halves(6, START16), halves(7, START16)], [near0, near1])
    (r5,) = up(after(f5, near1[1]), None, [halves(10, START8), halves(11, START8)], [near0, near1])
    far, r3, r4, r5 = lax.optimization_barrier((far, r3, r4, r5))
    s2, sent = up(
        f2,
        None,
        [("far", 1, NONE, 0), ("far", 2, NONE, 8)],
        [near0 + (far,), near1 + (far,)],
        level=2,
        inverse=[upper_inv],
        ways=16,
    )
    near2 = collected(sent, plane)
    (r4,) = up(after(r4, near2[0]), None, [halves(8, START16)], [(near2[0], near2[1])])
    s3, sent = up(r3, None, [halves(5)], [near2], level=3, inverse=[upper_inv], ways=8)
    near3 = collected(sent, square)
    (r5,) = up(after(r5, near3[0]), None, [halves(12, START8)], [near2])
    near3 = (near3[0], after(near3[1], r5))
    s4, sent = up(r4, None, [halves(9)], [near3], level=4, inverse=[upper_inv], ways=8)
    near4 = (spread(sent, (1, 2, 4)),)
    return last_update(
        me,
        table,
        upper_off,
        r5,
        [halves(13, START8IN16), ("one", 14, NONE, 0)],
        [near3, near4],
        upper_inv,
        [s0, s1, s2, s3, s4],
    )


def solution(mesh):
    return jax.shard_map(
        on_device,
        mesh=mesh,
        in_specs=(
            P(None, ("group", "sub"), None, None),
            P(None, ("group", "sub"), None, None),
            P(None, ("group", "sub"), None, None),
            P(None, ("group", "sub"), None, None, None),
            P(None, ("group", "sub"), None, None, None),
            P(None, ("group", "sub"), None),
            P(None, ("group", "sub"), None),
        ),
        out_specs=P(None, ("group", "sub"), None, None),
        check_vma=False,
    )
```

```python
import functools

import jax
import jax.numpy as jnp
from jax import lax
from jax.experimental import pallas as pl
from jax.experimental.pallas import tpu as pltpu
from jax.sharding import PartitionSpec as P

DUO_BITS = 7
DUO_BLOCKS = 1 << DUO_BITS
VMEM = pl.BlockSpec(memory_space=pltpu.VMEM)
SMEM = pl.BlockSpec(memory_space=pltpu.SMEM)
HBM = pl.BlockSpec(memory_space=pl.ANY)
PARAMS = pltpu.CompilerParams(vmem_limit_bytes=8 * 2**20)


def span(masks, count):
    groups, seen = [], set()
    for first in range(count):
        if first not in seen:
            group = [first]
            for mask in masks:
                group = group + [member ^ mask for member in group]
            seen.update(group)
            groups.append(sorted(group))
    return groups


def swapped(block, axis, mask):
    return lax.ppermute(block, axis, [(i, i ^ mask) for i in range(lax.axis_size(axis))])


def spread(copies, masks):
    axes = ("group", "sub")
    groups = span(masks, lax.axis_size("group") * lax.axis_size("sub"))
    return lax.all_to_all(copies, axes, 0, 0, tiled=True, axis_index_groups=groups)


def collected(copies, masks):
    own = spread(copies, masks)
    return own, swapped(own, "sub", 1)


def after(value, *others):
    return lax.optimization_barrier((value,) + others)[0]


def in_vmem(value):
    return pltpu.with_memory_space_constraint(value, pltpu.VMEM)


def in_smem(value):
    return pltpu.with_memory_space_constraint(value, pltpu.SMEM)


def in_hbm(value):
    return pltpu.with_memory_space_constraint(value, pltpu.HBM)


(CORE, DUO, PLANE64, SIXTEEN64, EIGHT64, SIXTEEN32, EIGHT32, EIGHT16, NONE) = range(9)
ACROSS, MATE, MATE_ACROSS = range(3)


def positions(sub, group):
    sixteen, eight = (sub >> 4) * 32, (sub >> 3) * 16
    plane = (group & 1) * 64
    return jnp.stack(
        [
            sub & 1,
            (group >> 1) & 1,
            plane,
            plane + sixteen,
            plane + eight,
            sixteen,
            eight,
            (sub >> 3 & 1) * 16,
        ]
    )


def block(own, other, local, core):
    index = (local >> 2 << 1) | (local & 1)
    return jnp.where((local >> 1 & 1) == core, own[index], other[index])


def read(kind, start, refs, me, wanted, slot):
    if kind == "one":
        return refs[0][wanted]
    if kind == "halves":
        local = wanted if start == NONE else wanted + me[start]
        return block(refs[0], refs[1], local, me[CORE])
    near = mixed(refs[0], refs[1], wanted & DUO_BLOCKS - 1, me[CORE], start + slot)
    if kind == "core":
        return near
    return jnp.where(wanted >> DUO_BITS == me[DUO], near, refs[2][slot])


def mixed(own, sent, local, core, slot):
    index = (local >> 2 << 1) | (local & 1)
    return jnp.where((local >> 1 & 1) == core, own[index], sent[slot])


def send(ref, j, value):
    value = value.astype(jnp.bfloat16)
    for way in range(ref.shape[0] // 2):
        ref[2 * way + j] = value


FIRST = (14, 13, 9, 12, 8, 5)
SECOND = (11, 7, 4, 2)
BUFFERS = {"one": 1, "halves": 2, "core": 2, "far": 3}


def coupled(total, j, plan, near, side, kept, me, table, off):
    for (kind, p, start), buffers in zip(plan, near):
        at = kept.index(p) if kept else p
        matrices = off[at, j].reshape(512, 128)
        picked = [
            read(kind, start, buffers, me, table[2 * side + j, n, p], j * 4 + n)
            for n in range(4)
        ]
        total = total - jnp.dot(
            jnp.concatenate(picked, 1), matrices, preferred_element_type=jnp.float32
        )
    return total


def times(total, matrix):
    return jnp.dot(total.astype(jnp.bfloat16), matrix, preferred_element_type=jnp.float32)


def update_kernel(plan, side, kept, first, level, inverses, ways, me, table, off, base, *refs):
    refs = list(refs)
    near = [[refs.pop(0) for _ in range(BUFFERS[entry[0]])] for entry in plan]
    inverse = [refs.pop(0) for _ in range(inverses)]
    for j in range(2):
        total = base[first, j] if first is not None else base[j]
        total = coupled(total, j, plan, near, side, kept, me, table, off)
        if not inverses:
            refs[0][j] = total
        for matrix in inverse:
            total = times(total, matrix[level, j])
        if inverses:
            refs[0][j] = total
        if ways:
            send(refs[-1], j, total)


def update(me, table, off, base, first, plan, near, side, level=0, inverse=(), ways=0, kept=None):
    shape = (2,) + base.shape[-2:]
    shapes = [jax.ShapeDtypeStruct(shape, jnp.float32)]
    if ways:
        shapes.append(jax.ShapeDtypeStruct((2 * ways,) + shape[1:], jnp.bfloat16))
    arguments = [in_smem(me), in_smem(table), in_vmem(off), in_vmem(base)]
    for buffers in near:
        arguments += list(buffers)
    arguments += [in_vmem(matrix) for matrix in inverse]
    products = 2 * (4 * len(plan) + len(inverse))
    return pl.pallas_call(
        functools.partial(
            update_kernel, tuple(plan), side, kept, first, level, len(inverse), ways
        ),
        out_shape=shapes,
        in_specs=[SMEM, SMEM] + [VMEM] * (len(arguments) - 2),
        out_specs=[VMEM] * len(shapes),
        compiler_params=PARAMS,
        cost_estimate=pl.CostEstimate(
            flops=products * 2 * 32 * 128 * 128, bytes_accessed=products * 32768, transcendentals=0
        ),
    )(*arguments)


def first_kernel(level, base, matrix, out, low, right, inverse, sems):
    copies = [
        pltpu.make_async_copy(base.at[level], right, sems.at[0]),
        pltpu.make_async_copy(matrix.at[level], inverse, sems.at[1]),
    ]
    for copy in copies:
        copy.start()
    for copy in copies:
        copy.wait()
    for j in range(2):
        total = times(right[j], inverse[j])
        out[j] = total
        send(low, j, total)


def first_update(right_sides, inverse, ways):
    levels = right_sides.shape[0]
    shape, matrix = right_sides.shape[1:], inverse.shape[1:]
    return pl.pallas_call(
        functools.partial(first_kernel, levels - 1),
        out_shape=[
            jax.ShapeDtypeStruct(shape, jnp.float32),
            jax.ShapeDtypeStruct((2 * ways,) + shape[1:], jnp.bfloat16),
        ],
        in_specs=[HBM, HBM],
        out_specs=[VMEM, VMEM],
        scratch_shapes=[
            pltpu.VMEM(shape, jnp.float32),
            pltpu.VMEM(matrix, jnp.bfloat16),
            pltpu.SemaphoreType.DMA((2,)),
        ],
        compiler_params=PARAMS,
    )(in_hbm(right_sides), in_hbm(inverse))


def last_kernel(plan, level, me, table, off, base, *refs):
    refs = list(refs)
    near = [[refs.pop(0) for _ in range(BUFFERS[entry[0]])] for entry in plan]
    inverse = refs.pop(0)
    out, result, sems = refs[-3:]
    copies = [
        pltpu.make_async_copy(ref, out.at[at], sems.at[at]) for at, ref in enumerate(refs[:-3])
    ]
    for copy in copies:
        copy.start()
    for j in range(2):
        total = coupled(base[j], j, plan, near, 1, None, me, table, off)
        result[j] = times(total, inverse[level, j])
    copies.append(pltpu.make_async_copy(result, out.at[level], sems.at[level]))
    copies[-1].start()
    for copy in copies:
        copy.wait()


def last_update(me, table, off, base, plan, near, inverse, solved):
    levels = len(solved) + 1
    arguments = [in_smem(me), in_smem(table), in_vmem(off), in_vmem(base)]
    for buffers in near:
        arguments += list(buffers)
    arguments += [in_vmem(inverse)] + [in_vmem(value) for value in solved]
    return pl.pallas_call(
        functools.partial(last_kernel, tuple(plan), levels - 1),
        out_shape=jax.ShapeDtypeStruct((levels,) + base.shape, jnp.float32),
        in_specs=[SMEM, SMEM] + [VMEM] * (len(arguments) - 2),
        out_specs=HBM,
        scratch_shapes=[
            pltpu.VMEM(base.shape, jnp.float32),
            pltpu.SemaphoreType.DMA((levels,)),
        ],
        compiler_params=PARAMS,
    )(*arguments)


def stage_kernel(plan, count, *refs):
    outs, sems = refs[count:-1], refs[-1]
    copies = []
    for which, place, rows, out, at in plan:
        target = outs[out] if at is None else outs[out].at[pl.ds(at, len(rows) if rows else place)]
        for offset, row in enumerate(rows or (None,)):
            source = refs[which] if row is None else refs[which].at[row]
            if row is not None:
                target = outs[out].at[at + offset]
            copies.append(pltpu.make_async_copy(source, target, sems.at[len(copies)]))
    for copy in copies:
        copy.start()
    for copy in copies:
        copy.wait()


def staged(*items):
    arrays, shapes, specs, plan, copies = [], [], [], [], 0
    for out, (space, parts, rows) in enumerate(items):
        at = 0
        for part in parts:
            size = part.shape[0]
            whole = rows is None and len(parts) == 1
            plan.append((len(arrays), size, rows, out, None if whole else at))
            arrays.append(in_hbm(part))
            copies += len(rows) if rows else 1
            at += len(rows) if rows else size
        shapes.append(space((at,) + parts[0].shape[1:], parts[0].dtype))
        specs.append(VMEM if space is pltpu.VMEM else SMEM)
    moved = sum(shape.size if hasattr(shape, "size") else 0 for shape in shapes)
    return pl.pallas_call(
        functools.partial(stage_kernel, tuple(plan), len(arrays)),
        out_shape=shapes,
        in_specs=[HBM] * len(arrays),
        out_specs=specs,
        scratch_shapes=[pltpu.SemaphoreType.DMA((copies,))],
        compiler_params=PARAMS,
        cost_estimate=pl.CostEstimate(
            flops=0, bytes_accessed=max(2 * moved, 4_000_000), transcendentals=0
        ),
    )(*arrays)


def pick_kernel(plan, side, me, table, own, *refs):
    sent, out = refs if len(refs) == 2 else (None, refs[0])
    for at, (peer, p) in enumerate(plan):
        for j in range(2):
            for n in range(4):
                local = table[peer, 2 * side + j, n, p] & DUO_BLOCKS - 1
                slot = 4 * j + n
                if sent is None:
                    out[8 * at + slot] = own[(local >> 2 << 1) | (local & 1)]
                else:
                    out[8 * at + slot] = mixed(own, sent, local, me[CORE], 8 + slot)


def pick(me, table, plan, side, own, *sent):
    return pl.pallas_call(
        functools.partial(pick_kernel, tuple(plan), side),
        out_shape=jax.ShapeDtypeStruct((8 * len(plan),) + own.shape[1:], jnp.bfloat16),
        in_specs=[SMEM, SMEM, VMEM] + [VMEM] * len(sent),
        out_specs=VMEM,
        compiler_params=PARAMS,
        cost_estimate=pl.CostEstimate(
            flops=0, bytes_accessed=131072 * len(plan), transcendentals=0
        ),
    )(in_smem(me), in_smem(table), own, *sent)


def halves(p, start=NONE):
    return ("halves", p, start)


def on_device(
    right_sides, lower_inv, upper_inv, lower_off, upper_off, lower_pattern, upper_pattern
):
    sub, group = lax.axis_index("sub"), lax.axis_index("group")
    square, plane, duo = (2, 4, 8), (2, 4, 8, 16), (2, 4, 8, 16, 32)

    tables = [x.transpose(1, 2, 0) for x in (lower_pattern, upper_pattern)]
    mine = jnp.concatenate(tables)
    across = swapped(mine, "group", 2)

    f5, sent = first_update(right_sides, lower_inv, 8)
    right, lower_inv, off_first, table, me = staged(
        (pltpu.VMEM, [after(right_sides, sent)], None),
        (pltpu.VMEM, [lower_inv], None),
        (pltpu.VMEM, [lower_off], FIRST),
        (pltpu.SMEM, tables, None),
        (pltpu.SMEM, [positions(sub, group)], None),
    )
    near5, across, me = lax.optimization_barrier((spread(sent, (1, 2, 4)), across, me))
    near5 = (near5,)
    low = functools.partial(update, me, table, off_first, side=0, kept=FIRST)

    f4, sent = low(right, 4, [("one", 14, NONE)], [near5], level=4, inverse=[lower_inv], ways=8)
    near4 = collected(sent, square)
    mates = swapped(after(jnp.stack([mine, across]), near4[0]), "sub", 1)
    (r3,) = low(after(right, near4[0]), 3, [("one", 13, NONE)], [near5])
    (off_second,) = staged((pltpu.VMEM, [after(lower_off, near4[0])], SECOND))
    near4 = (near4[0], after(near4[1], off_second, mates))
    f3, sent = low(r3, None, [halves(9)], [near4], level=3, inverse=[lower_inv], ways=16)
    near3 = collected(sent, plane)
    (peers,) = staged((pltpu.SMEM, [after(across[None], near3[0]), mates], None))
    (r2,) = low(after(right, near3[0]), 2, [("one", 12, NONE), halves(8)], [near5, near4])
    near3 = (near3[0], after(near3[1], peers))
    f2, sent = low(r2, None, [halves(5)], [near3], level=2, inverse=[lower_inv], ways=32)
    low = functools.partial(update, me, table, off_second, side=0, kept=SECOND)
    own2 = spread(sent, duo)
    near2 = (own2, swapped(pick(me, peers, [(MATE, 2), (MATE, 1)], 0, own2), "sub", 1))
    (r1,) = low(
        after(right, own2), 1, [("one", 11, NONE), halves(7), halves(4)], [near5, near4, near3]
    )
    f1, sent = low(r1, None, [("core", 2, 0)], [near2], level=1, inverse=[lower_inv], ways=32)
    own1 = spread(sent, duo)
    near1 = (own1, swapped(pick(me, peers, [(MATE, 0), (MATE_ACROSS, 0)], 0, own1), "sub", 1))
    sent = pick(me, peers, [(ACROSS, 0)], 0, *near1)
    far = swapped(sent, "group", 2)
    lower_off, upper_inv, upper_first = staged(
        (pltpu.VMEM, [after(lower_off, sent)], None),
        (pltpu.VMEM, [upper_inv], None),
        (pltpu.VMEM, [upper_off], (0,)),
    )
    low = functools.partial(update, me, table, lower_off, side=0)
    (r0,) = low(
        right,
        0,
        [("one", 10, NONE), halves(6), halves(3), ("core", 1, 8)],
        [near5, near4, near3, near2],
    )
    far, upper_first = lax.optimization_barrier((far, upper_first))
    s0, sent = low(
        r0,
        None,
        [("far", 0, 0)],
        [near1 + (far,)],
        level=0,
        inverse=[lower_inv, upper_inv],
        ways=32,
    )

    own0 = spread(sent, duo)
    near0 = (own0, swapped(pick(me, peers, [(MATE, 0), (MATE_ACROSS, 0)], 1, own0), "sub", 1))
    sent = pick(me, peers, [(ACROSS, 0)], 1, *near0)
    far = swapped(sent, "group", 2)
    (upper_off,) = staged((pltpu.VMEM, [after(upper_off, sent)], None))
    other0 = swapped(after(own0, sent), "sub", 1)
    far, upper_off, other0 = lax.optimization_barrier((far, upper_off, other0))
    up = functools.partial(update, me, table, upper_off, side=1)
    s1, sent = up(
        f1, None, [("far", 0, 0)], [near0 + (far,)], level=1, inverse=[upper_inv], ways=32
    )
    near0 = (own0, other0)
    own1 = spread(sent, duo)
    near1 = (own1, swapped(pick(me, peers, [(MATE, 2)], 1, own1), "sub", 1))
    (r2,) = up(after(f2, own1), None, [halves(1)], [near0])
    s2, sent = up(r2, None, [("core", 2, 0)], [near1], level=2, inverse=[upper_inv], ways=16)
    near1 = (own1, swapped(after(own1, sent), "sub", 1))
    near2 = collected(sent, plane)
    (r3,) = up(
        after(f3, near2[0]), None, [halves(3, PLANE64), halves(4, PLANE64)], [near0, near1]
    )
    s3, sent = up(r3, None, [halves(5)], [near2], level=3, inverse=[upper_inv], ways=8)
    near3 = collected(sent, square)
    (r4,) = up(
        after(f4, near3[0]),
        None,
        [halves(6, SIXTEEN64), halves(7, SIXTEEN64), halves(8, SIXTEEN32)],
        [near0, near1, near2],
    )
    (r5,) = up(
        after(f5, near3[0]),
        None,
        [halves(10, EIGHT64), halves(11, EIGHT64), halves(12, EIGHT32)],
        [near0, near1, near2],
    )
    near3 = (near3[0], after(near3[1], r5))
    s4, sent = up(r4, None, [halves(9)], [near3], level=4, inverse=[upper_inv], ways=8)
    near4 = (spread(sent, (1, 2, 4)),)
    return last_update(
        me,
        table,
        upper_off,
        r5,
        [halves(13, EIGHT16), ("one", 14, NONE)],
        [near3, near4],
        upper_inv,
        [s0, s1, s2, s3, s4],
    )


def solution(mesh):
    return jax.shard_map(
        on_device,
        mesh=mesh,
        in_specs=(
            P(None, ("group", "sub"), None, None),
            P(None, ("group", "sub"), None, None),
            P(None, ("group", "sub"), None, None),
            P(None, ("group", "sub"), None, None, None),
            P(None, ("group", "sub"), None, None, None),
            P(None, ("group", "sub"), None),
            P(None, ("group", "sub"), None),
        ),
        out_specs=P(None, ("group", "sub"), None, None),
        check_vma=False,
    )
```

```python
import functools

import jax
import jax.numpy as jnp
from jax import lax
from jax.experimental import pallas as pl
from jax.experimental.pallas import tpu as pltpu
from jax.sharding import PartitionSpec as P

DUO_BITS = 7
DUO_BLOCKS = 1 << DUO_BITS
VMEM = pl.BlockSpec(memory_space=pltpu.VMEM)
SMEM = pl.BlockSpec(memory_space=pltpu.SMEM)
HBM = pl.BlockSpec(memory_space=pl.ANY)
PARAMS = pltpu.CompilerParams(vmem_limit_bytes=8 * 2**20)


def span(masks, count):
    groups, seen = [], set()
    for first in range(count):
        if first not in seen:
            group = [first]
            for mask in masks:
                group = group + [member ^ mask for member in group]
            seen.update(group)
            groups.append(sorted(group))
    return groups


def swapped(block, axis, mask):
    return lax.ppermute(block, axis, [(i, i ^ mask) for i in range(lax.axis_size(axis))])


def spread(copies, masks):
    axes = ("group", "sub")
    groups = span(masks, lax.axis_size("group") * lax.axis_size("sub"))
    return lax.all_to_all(copies, axes, 0, 0, tiled=True, axis_index_groups=groups)


def collected(copies, masks):
    own = spread(copies, masks)
    return own, swapped(own, "sub", 1)


def after(value, *others):
    return lax.optimization_barrier((value,) + others)[0]


def in_vmem(value):
    return pltpu.with_memory_space_constraint(value, pltpu.VMEM)


def in_smem(value):
    return pltpu.with_memory_space_constraint(value, pltpu.SMEM)


def in_hbm(value):
    return pltpu.with_memory_space_constraint(value, pltpu.HBM)


(CORE, DUO, PLANE64, SIXTEEN64, EIGHT64, SIXTEEN32, EIGHT32, EIGHT16, NONE) = range(9)
ACROSS, MATE, MATE_ACROSS = range(3)


def positions(sub, group):
    sixteen, eight = (sub >> 4) * 32, (sub >> 3) * 16
    plane = (group & 1) * 64
    return jnp.stack(
        [
            sub & 1,
            (group >> 1) & 1,
            plane,
            plane + sixteen,
            plane + eight,
            sixteen,
            eight,
            (sub >> 3 & 1) * 16,
        ]
    )


def block(own, other, local, core):
    index = (local >> 2 << 1) | (local & 1)
    return jnp.where((local >> 1 & 1) == core, own[index], other[index])


def read(kind, start, refs, me, wanted, slot):
    if kind == "one":
        return refs[0][wanted]
    if kind == "halves":
        local = wanted if start == NONE else wanted + me[start]
        return block(refs[0], refs[1], local, me[CORE])
    near = mixed(refs[0], refs[1], wanted & DUO_BLOCKS - 1, me[CORE], start + slot)
    if kind == "core":
        return near
    return jnp.where(wanted >> DUO_BITS == me[DUO], near, refs[2][slot])


def mixed(own, sent, local, core, slot):
    index = (local >> 2 << 1) | (local & 1)
    return jnp.where((local >> 1 & 1) == core, own[index], sent[slot])


def send(ref, totals):
    values = [total.astype(jnp.bfloat16) for total in totals]
    for way in range(ref.shape[0] // 2):
        for j in range(2):
            ref[2 * way + j] = values[j]


FIRST = (14, 13, 9, 12, 8, 5, 11, 7, 4, 2)
BUFFERS = {"one": 1, "halves": 2, "core": 2, "far": 3}


def coupled(total, j, plan, near, side, kept, me, table, off):
    for (kind, p, start), buffers in zip(plan, near):
        at = kept.index(p) if kept else p
        picked = [
            read(kind, start, buffers, me, table[2 * side + j, n, p], j * 4 + n) for n in range(4)
        ]
        total = total - jnp.dot(
            jnp.concatenate(picked, 1),
            off[at, j].reshape(512, 128),
            preferred_element_type=jnp.float32,
        )
    return total


def times(total, matrix):
    return jnp.dot(total.astype(jnp.bfloat16), matrix, preferred_element_type=jnp.float32)


def update_kernel(plan, side, kept, first, level, inverses, ways, me, table, off, base, *refs):
    refs = list(refs)
    near = [[refs.pop(0) for _ in range(BUFFERS[entry[0]])] for entry in plan]
    inverse = [refs.pop(0) for _ in range(inverses)]
    totals = [
        coupled(base[first, j] if first is not None else base[j], j, plan, near, side, kept, me, table, off)
        for j in range(2)
    ]
    for matrix in inverse:
        totals = [times(totals[j], matrix[level, j]) for j in range(2)]
    for j in range(2):
        refs[0][j] = totals[j]
    if ways:
        send(refs[-1], totals)


def update(me, table, off, base, first, plan, near, side, level=0, inverse=(), ways=0, kept=None):
    shape = (2,) + base.shape[-2:]
    shapes = [jax.ShapeDtypeStruct(shape, jnp.float32)]
    if ways:
        shapes.append(jax.ShapeDtypeStruct((2 * ways,) + shape[1:], jnp.bfloat16))
    arguments = [in_smem(me), in_smem(table), in_vmem(off), in_vmem(base)]
    for buffers in near:
        arguments += list(buffers)
    arguments += [in_vmem(matrix) for matrix in inverse]
    products = 2 * (4 * len(plan) + len(inverse))
    return pl.pallas_call(
        functools.partial(
            update_kernel, tuple(plan), side, kept, first, level, len(inverse), ways
        ),
        out_shape=shapes,
        in_specs=[SMEM, SMEM] + [VMEM] * (len(arguments) - 2),
        out_specs=[VMEM] * len(shapes),
        compiler_params=PARAMS,
        cost_estimate=pl.CostEstimate(
            flops=products * 2 * 32 * 128 * 128, bytes_accessed=products * 32768, transcendentals=0
        ),
    )(*arguments)


def first_kernel(level, base, matrix, lower, upper, out, low, joined, right, inverse, sems):
    rows = lower.shape[0]
    copies = [
        pltpu.make_async_copy(base.at[level], right, sems.at[0]),
        pltpu.make_async_copy(matrix.at[level], inverse, sems.at[1]),
        pltpu.make_async_copy(lower, joined.at[pl.ds(0, rows)], sems.at[2]),
        pltpu.make_async_copy(upper, joined.at[pl.ds(rows, rows)], sems.at[3]),
    ]
    for copy in copies:
        copy.start()
    copies[0].wait()
    copies[1].wait()
    totals = [times(right[j], inverse[j]) for j in range(2)]
    for j in range(2):
        out[j] = totals[j]
    send(low, totals)
    copies[2].wait()
    copies[3].wait()


def first_update(right_sides, inverse, lower, upper, ways):
    levels = right_sides.shape[0]
    shape, matrix = right_sides.shape[1:], inverse.shape[1:]
    return pl.pallas_call(
        functools.partial(first_kernel, levels - 1),
        out_shape=[
            jax.ShapeDtypeStruct(shape, jnp.float32),
            jax.ShapeDtypeStruct((2 * ways,) + shape[1:], jnp.bfloat16),
            jax.ShapeDtypeStruct((2 * lower.shape[0],) + lower.shape[1:], lower.dtype),
        ],
        in_specs=[HBM] * 4,
        out_specs=[VMEM] * 3,
        scratch_shapes=[
            pltpu.VMEM(shape, jnp.float32),
            pltpu.VMEM(matrix, jnp.bfloat16),
            pltpu.SemaphoreType.DMA((4,)),
        ],
        compiler_params=PARAMS,
    )(in_hbm(right_sides), in_hbm(inverse), in_hbm(lower), in_hbm(upper))


def last_kernel(plan, level, me, table, off, base, *refs):
    refs = list(refs)
    near = [[refs.pop(0) for _ in range(BUFFERS[entry[0]])] for entry in plan]
    inverse = refs.pop(0)
    out, result, sems = refs[-3:]
    copies = [
        pltpu.make_async_copy(ref, out.at[at], sems.at[at]) for at, ref in enumerate(refs[:-3])
    ]
    for copy in copies:
        copy.start()
    totals = [coupled(base[j], j, plan, near, 1, None, me, table, off) for j in range(2)]
    for j in range(2):
        result[j] = times(totals[j], inverse[level, j])
    copies.append(pltpu.make_async_copy(result, out.at[level], sems.at[level]))
    copies[-1].start()
    for copy in copies:
        copy.wait()


def last_update(me, table, off, base, plan, near, inverse, solved):
    levels = len(solved) + 1
    arguments = [in_smem(me), in_smem(table), in_vmem(off), in_vmem(base)]
    for buffers in near:
        arguments += list(buffers)
    arguments += [in_vmem(inverse)] + [in_vmem(value) for value in solved]
    return pl.pallas_call(
        functools.partial(last_kernel, tuple(plan), levels - 1),
        out_shape=jax.ShapeDtypeStruct((levels,) + base.shape, jnp.float32),
        in_specs=[SMEM, SMEM] + [VMEM] * (len(arguments) - 2),
        out_specs=HBM,
        scratch_shapes=[
            pltpu.VMEM(base.shape, jnp.float32),
            pltpu.SemaphoreType.DMA((levels,)),
        ],
        compiler_params=PARAMS,
    )(*arguments)


def stage_kernel(plan, count, *refs):
    outs, sems = refs[count:-1], refs[-1]
    copies = []
    for which, place, rows, out, at in plan:
        target = outs[out] if at is None else outs[out].at[pl.ds(at, len(rows) if rows else place)]
        for offset, row in enumerate(rows or (None,)):
            source = refs[which] if row is None else refs[which].at[row]
            if row is not None:
                target = outs[out].at[at + offset]
            copies.append(pltpu.make_async_copy(source, target, sems.at[len(copies)]))
    for copy in copies:
        copy.start()
    for copy in copies:
        copy.wait()


def staged(*items):
    arrays, shapes, specs, plan, copies = [], [], [], [], 0
    for out, (space, parts, rows) in enumerate(items):
        at = 0
        for part in parts:
            size = part.shape[0]
            whole = rows is None and len(parts) == 1
            plan.append((len(arrays), size, rows, out, None if whole else at))
            arrays.append(part if part.ndim < 3 else in_hbm(part))
            copies += len(rows) if rows else 1
            at += len(rows) if rows else size
        shapes.append(space((at,) + parts[0].shape[1:], parts[0].dtype))
        specs.append(VMEM if space is pltpu.VMEM else SMEM)
    moved = sum(shape.size if hasattr(shape, "size") else 0 for shape in shapes)
    return pl.pallas_call(
        functools.partial(stage_kernel, tuple(plan), len(arrays)),
        out_shape=shapes,
        in_specs=[HBM] * len(arrays),
        out_specs=specs,
        scratch_shapes=[pltpu.SemaphoreType.DMA((copies,))],
        compiler_params=PARAMS,
        cost_estimate=pl.CostEstimate(
            flops=0, bytes_accessed=max(2 * moved, 4_000_000), transcendentals=0
        ),
    )(*arrays)


def pick_kernel(plan, side, me, table, own, *refs):
    sent, out = refs if len(refs) == 2 else (None, refs[0])
    for at, (peer, p) in enumerate(plan):
        for j in range(2):
            for n in range(4):
                local = table[peer, 2 * side + j, n, p] & DUO_BLOCKS - 1
                slot = 4 * j + n
                if sent is None:
                    out[8 * at + slot] = own[(local >> 2 << 1) | (local & 1)]
                else:
                    out[8 * at + slot] = mixed(own, sent, local, me[CORE], 8 + slot)


def pick(me, table, plan, side, own, *sent):
    return pl.pallas_call(
        functools.partial(pick_kernel, tuple(plan), side),
        out_shape=jax.ShapeDtypeStruct((8 * len(plan),) + own.shape[1:], jnp.bfloat16),
        in_specs=[SMEM, SMEM, VMEM] + [VMEM] * len(sent),
        out_specs=VMEM,
        compiler_params=PARAMS,
        cost_estimate=pl.CostEstimate(
            flops=0, bytes_accessed=131072 * len(plan), transcendentals=0
        ),
    )(in_smem(me), in_smem(table), own, *sent)


def halves(p, start=NONE):
    return ("halves", p, start)


def on_device(
    right_sides, lower_inv, upper_inv, lower_off, upper_off, lower_pattern, upper_pattern
):
    sub, group = lax.axis_index("sub"), lax.axis_index("group")
    square, plane, duo = (2, 4, 8), (2, 4, 8, 16), (2, 4, 8, 16, 32)

    tables = [x.transpose(1, 2, 0) for x in (lower_pattern, upper_pattern)]
    f5, sent, mine = first_update(right_sides, lower_inv, *tables, 8)
    across = swapped(mine, "group", 2)
    right, lower_inv, off_first, table, me = staged(
        (pltpu.VMEM, [after(right_sides, sent)], None),
        (pltpu.VMEM, [lower_inv], None),
        (pltpu.VMEM, [lower_off], FIRST),
        (pltpu.SMEM, tables, None),
        (pltpu.SMEM, [positions(sub, group)], None),
    )
    near5, across, me = lax.optimization_barrier((spread(sent, (1, 2, 4)), across, me))
    near5 = (near5,)
    low = functools.partial(update, me, table, off_first, side=0, kept=FIRST)

    f4, sent = low(right, 4, [("one", 14, NONE)], [near5], level=4, inverse=[lower_inv], ways=8)
    near4 = collected(sent, square)
    mates = swapped(after(jnp.stack([mine, across]), near4[0]), "sub", 1)
    (r3,) = low(after(right, near4[0]), 3, [("one", 13, NONE)], [near5])
    near4 = (near4[0], after(near4[1], mates))
    f3, sent = low(r3, None, [halves(9)], [near4], level=3, inverse=[lower_inv], ways=16)
    near3 = collected(sent, plane)
    (peers,) = staged((pltpu.SMEM, [after(across[None], near3[0]), mates], None))
    (r2,) = low(after(right, near3[0]), 2, [("one", 12, NONE), halves(8)], [near5, near4])
    near3 = (near3[0], after(near3[1], peers))
    f2, sent = low(r2, None, [halves(5)], [near3], level=2, inverse=[lower_inv], ways=32)
    own2 = spread(sent, duo)
    near2 = (own2, swapped(pick(me, peers, [(MATE, 2), (MATE, 1)], 0, own2), "sub", 1))
    (r1,) = low(
        after(right, own2), 1, [("one", 11, NONE), halves(7), halves(4)], [near5, near4, near3]
    )
    f1, sent = low(r1, None, [("core", 2, 0)], [near2], level=1, inverse=[lower_inv], ways=32)
    own1 = spread(sent, duo)
    near1 = (own1, swapped(pick(me, peers, [(MATE, 0), (MATE_ACROSS, 0)], 0, own1), "sub", 1))
    sent = pick(me, peers, [(ACROSS, 0)], 0, *near1)
    far = swapped(sent, "group", 2)
    lower_off, upper_inv, upper_first = staged(
        (pltpu.VMEM, [after(lower_off, sent)], None),
        (pltpu.VMEM, [upper_inv], None),
        (pltpu.VMEM, [upper_off], (0,)),
    )
    low = functools.partial(update, me, table, lower_off, side=0)
    (r0,) = low(
        right,
        0,
        [("one", 10, NONE), halves(6), halves(3), ("core", 1, 8)],
        [near5, near4, near3, near2],
    )
    far, upper_first = lax.optimization_barrier((far, upper_first))
    s0, sent = low(
        r0,
        None,
        [("far", 0, 0)],
        [near1 + (far,)],
        level=0,
        inverse=[lower_inv, upper_inv],
        ways=32,
    )

    own0 = spread(sent, duo)
    near0 = (own0, swapped(pick(me, peers, [(MATE, 0), (MATE_ACROSS, 0)], 1, own0), "sub", 1))
    sent = pick(me, peers, [(ACROSS, 0)], 1, *near0)
    far = swapped(sent, "group", 2)
    (upper_off,) = staged((pltpu.VMEM, [after(upper_off, sent)], None))
    other0 = swapped(after(own0, sent), "sub", 1)
    far, upper_off, other0 = lax.optimization_barrier((far, upper_off, other0))
    up = functools.partial(update, me, table, upper_off, side=1)
    s1, sent = up(
        f1, None, [("far", 0, 0)], [near0 + (far,)], level=1, inverse=[upper_inv], ways=32
    )
    near0 = (own0, other0)
    own1 = spread(sent, duo)
    near1 = (own1, swapped(pick(me, peers, [(MATE, 2)], 1, own1), "sub", 1))
    (r2,) = up(after(f2, own1), None, [halves(1)], [near0])
    s2, sent = up(r2, None, [("core", 2, 0)], [near1], level=2, inverse=[upper_inv], ways=16)
    near1 = (own1, swapped(after(own1, sent), "sub", 1))
    near2 = collected(sent, plane)
    (r3,) = up(
        after(f3, near2[0]), None, [halves(3, PLANE64), halves(4, PLANE64)], [near0, near1]
    )
    s3, sent = up(r3, None, [halves(5)], [near2], level=3, inverse=[upper_inv], ways=8)
    near3 = collected(sent, square)
    (r4,) = up(
        after(f4, near3[0]),
        None,
        [halves(6, SIXTEEN64), halves(7, SIXTEEN64), halves(8, SIXTEEN32)],
        [near0, near1, near2],
    )
    (r5,) = up(
        after(f5, near3[0]),
        None,
        [halves(10, EIGHT64), halves(11, EIGHT64), halves(12, EIGHT32)],
        [near0, near1, near2],
    )
    near3 = (near3[0], after(near3[1], r5))
    s4, sent = up(r4, None, [halves(9)], [near3], level=4, inverse=[upper_inv], ways=8)
    near4 = (spread(sent, (1, 2, 4)),)
    return last_update(
        me,
        table,
        upper_off,
        r5,
        [halves(13, EIGHT16), ("one", 14, NONE)],
        [near3, near4],
        upper_inv,
        [s0, s1, s2, s3, s4],
    )


def solution(mesh):
    return jax.shard_map(
        on_device,
        mesh=mesh,
        in_specs=(
            P(None, ("group", "sub"), None, None),
            P(None, ("group", "sub"), None, None),
            P(None, ("group", "sub"), None, None),
            P(None, ("group", "sub"), None, None, None),
            P(None, ("group", "sub"), None, None, None),
            P(None, ("group", "sub"), None),
            P(None, ("group", "sub"), None),
        ),
        out_specs=P(None, ("group", "sub"), None, None),
        check_vma=False,
    )
```

```python
import functools

import jax
import jax.numpy as jnp
from jax import lax
from jax.experimental import pallas as pl
from jax.experimental.pallas import tpu as pltpu
from jax.sharding import PartitionSpec as P

DUO_BITS = 7
DUO_BLOCKS = 1 << DUO_BITS
VMEM = pl.BlockSpec(memory_space=pltpu.VMEM)
SMEM = pl.BlockSpec(memory_space=pltpu.SMEM)
HBM = pl.BlockSpec(memory_space=pl.ANY)
PARAMS = pltpu.CompilerParams(vmem_limit_bytes=8 * 2**20)


def span(masks, count):
    groups, seen = [], set()
    for first in range(count):
        if first not in seen:
            group = [first]
            for mask in masks:
                group = group + [member ^ mask for member in group]
            seen.update(group)
            groups.append(sorted(group))
    return groups


def swapped(block, axis, mask):
    return lax.ppermute(block, axis, [(i, i ^ mask) for i in range(lax.axis_size(axis))])


def spread(copies, masks):
    axes = ("group", "sub")
    groups = span(masks, lax.axis_size("group") * lax.axis_size("sub"))
    return lax.all_to_all(copies, axes, 0, 0, tiled=True, axis_index_groups=groups)


def collected(copies, masks):
    own = spread(copies, masks)
    return own, swapped(own, "sub", 1)


def after(value, *others):
    return lax.optimization_barrier((value,) + others)[0]


def in_vmem(value):
    return pltpu.with_memory_space_constraint(value, pltpu.VMEM)


def in_smem(value):
    return pltpu.with_memory_space_constraint(value, pltpu.SMEM)


def in_hbm(value):
    return pltpu.with_memory_space_constraint(value, pltpu.HBM)


(CORE, DUO, PLANE64, SIXTEEN64, EIGHT64, SIXTEEN32, EIGHT32, EIGHT16, NONE) = range(9)
ACROSS, MATE, MATE_ACROSS = range(3)


def positions(sub, group):
    sixteen, eight = (sub >> 4) * 32, (sub >> 3) * 16
    plane = (group & 1) * 64
    return jnp.stack(
        [
            sub & 1,
            (group >> 1) & 1,
            plane,
            plane + sixteen,
            plane + eight,
            sixteen,
            eight,
            (sub >> 3 & 1) * 16,
        ]
    )


def block(own, other, local, core):
    index = (local >> 2 << 1) | (local & 1)
    return jnp.where((local >> 1 & 1) == core, own[index], other[index])


def read(kind, start, refs, me, wanted, slot):
    if kind == "one":
        return refs[0][wanted]
    if kind == "halves":
        local = wanted if start == NONE else wanted + me[start]
        return block(refs[0], refs[1], local, me[CORE])
    near = mixed(refs[0], refs[1], wanted & DUO_BLOCKS - 1, me[CORE], start + slot)
    if kind == "core":
        return near
    return jnp.where(wanted >> DUO_BITS == me[DUO], near, refs[2][slot])


def mixed(own, sent, local, core, slot):
    index = (local >> 2 << 1) | (local & 1)
    return jnp.where((local >> 1 & 1) == core, own[index], sent[slot])


def send(ref, totals):
    values = [total.astype(jnp.bfloat16) for total in totals]
    for way in range(ref.shape[0] // 2):
        for j in range(2):
            ref[2 * way + j] = values[j]


FIRST = (14, 13, 9, 12, 8, 5, 11, 7, 4, 2)
BUFFERS = {"one": 1, "halves": 2, "core": 2, "far": 3}


def coupled(total, j, plan, near, side, kept, me, table, off):
    for (kind, p, start), buffers in zip(plan, near):
        at = kept.index(p) if kept else p
        picked = [
            read(kind, start, buffers, me, table[2 * side + j, n, p], j * 4 + n) for n in range(4)
        ]
        total = total - jnp.dot(
            jnp.concatenate(picked, 1),
            off[at, j].reshape(512, 128),
            preferred_element_type=jnp.float32,
        )
    return total


def times(total, matrix):
    return jnp.dot(total.astype(jnp.bfloat16), matrix, preferred_element_type=jnp.float32)


def update_kernel(plan, side, kept, first, level, inverses, ways, me, table, off, base, *refs):
    refs = list(refs)
    near = [[refs.pop(0) for _ in range(BUFFERS[entry[0]])] for entry in plan]
    inverse = [refs.pop(0) for _ in range(inverses)]
    totals = [
        coupled(base[first, j] if first is not None else base[j], j, plan, near, side, kept, me, table, off)
        for j in range(2)
    ]
    for matrix in inverse:
        totals = [times(totals[j], matrix[level, j]) for j in range(2)]
    for j in range(2):
        refs[0][j] = totals[j]
    if ways:
        send(refs[-1], totals)


def update(me, table, off, base, first, plan, near, side, level=0, inverse=(), ways=0, kept=None):
    shape = (2,) + base.shape[-2:]
    shapes = [jax.ShapeDtypeStruct(shape, jnp.float32)]
    if ways:
        shapes.append(jax.ShapeDtypeStruct((2 * ways,) + shape[1:], jnp.bfloat16))
    arguments = [in_smem(me), in_smem(table), in_vmem(off), in_vmem(base)]
    for buffers in near:
        arguments += list(buffers)
    arguments += [in_vmem(matrix) for matrix in inverse]
    products = 2 * (4 * len(plan) + len(inverse))
    return pl.pallas_call(
        functools.partial(
            update_kernel, tuple(plan), side, kept, first, level, len(inverse), ways
        ),
        out_shape=shapes,
        in_specs=[SMEM, SMEM] + [VMEM] * (len(arguments) - 2),
        out_specs=[VMEM] * len(shapes),
        compiler_params=PARAMS,
        cost_estimate=pl.CostEstimate(
            flops=products * 2 * 32 * 128 * 128, bytes_accessed=products * 32768, transcendentals=0
        ),
    )(*arguments)


def premultiply_kernel(entries, kept, count, off, *refs):
    out = refs[count]
    for at, (p, level) in enumerate(entries):
        for j in range(2):
            value = off[kept.index(p) if kept else p, j].reshape(512, 128)
            for matrix in refs[:count]:
                value = times(value, matrix[level, j]).astype(jnp.bfloat16)
            out[at, j] = value.reshape(out.shape[2:])


def premultiplied(off, kept, entries, matrices):
    return pl.pallas_call(
        functools.partial(premultiply_kernel, tuple(entries), kept, len(matrices)),
        out_shape=pltpu.VMEM((len(entries),) + off.shape[1:], off.dtype),
        in_specs=[VMEM] * (1 + len(matrices)),
        out_specs=VMEM,
        compiler_params=PARAMS,
        cost_estimate=pl.CostEstimate(
            flops=len(entries) * len(matrices) * 4 * 512 * 128 * 128,
            bytes_accessed=len(entries) * 524288,
            transcendentals=0,
        ),
    )(in_vmem(off), *[in_vmem(matrix) for matrix in matrices])


def first_kernel(level, base, matrix, lower, upper, out, low, joined, right, inverse, sems):
    rows = lower.shape[0]
    copies = [
        pltpu.make_async_copy(base.at[level], right, sems.at[0]),
        pltpu.make_async_copy(matrix.at[level], inverse, sems.at[1]),
        pltpu.make_async_copy(lower, joined.at[pl.ds(0, rows)], sems.at[2]),
        pltpu.make_async_copy(upper, joined.at[pl.ds(rows, rows)], sems.at[3]),
    ]
    for copy in copies:
        copy.start()
    copies[0].wait()
    copies[1].wait()
    totals = [times(right[j], inverse[j]) for j in range(2)]
    for j in range(2):
        out[j] = totals[j]
    send(low, totals)
    copies[2].wait()
    copies[3].wait()


def first_update(right_sides, inverse, lower, upper, ways):
    levels = right_sides.shape[0]
    shape, matrix = right_sides.shape[1:], inverse.shape[1:]
    return pl.pallas_call(
        functools.partial(first_kernel, levels - 1),
        out_shape=[
            jax.ShapeDtypeStruct(shape, jnp.float32),
            jax.ShapeDtypeStruct((2 * ways,) + shape[1:], jnp.bfloat16),
            jax.ShapeDtypeStruct((2 * lower.shape[0],) + lower.shape[1:], lower.dtype),
        ],
        in_specs=[HBM] * 4,
        out_specs=[VMEM] * 3,
        scratch_shapes=[
            pltpu.VMEM(shape, jnp.float32),
            pltpu.VMEM(matrix, jnp.bfloat16),
            pltpu.SemaphoreType.DMA((4,)),
        ],
        compiler_params=PARAMS,
    )(in_hbm(right_sides), in_hbm(inverse), in_hbm(lower), in_hbm(upper))


def last_kernel(plan, kept, me, table, off, base, *refs):
    refs = list(refs)
    near = [[refs.pop(0) for _ in range(BUFFERS[entry[0]])] for entry in plan]
    out, result, sems = refs[-3:]
    solved = refs[:-3]
    copies = [pltpu.make_async_copy(ref, out.at[at], sems.at[at]) for at, ref in enumerate(solved)]
    for copy in copies:
        copy.start()
    totals = [coupled(base[j], j, plan, near, 1, kept, me, table, off) for j in range(2)]
    for j in range(2):
        result[j] = totals[j]
    level = len(solved)
    copies.append(pltpu.make_async_copy(result, out.at[level], sems.at[level]))
    copies[-1].start()
    for copy in copies:
        copy.wait()


def last_update(me, table, off, base, plan, near, kept, solved):
    levels = len(solved) + 1
    arguments = [in_smem(me), in_smem(table), in_vmem(off), in_vmem(base)]
    for buffers in near:
        arguments += list(buffers)
    arguments += [in_vmem(value) for value in solved]
    return pl.pallas_call(
        functools.partial(last_kernel, tuple(plan), kept),
        out_shape=jax.ShapeDtypeStruct((levels,) + base.shape, jnp.float32),
        in_specs=[SMEM, SMEM] + [VMEM] * (len(arguments) - 2),
        out_specs=HBM,
        scratch_shapes=[
            pltpu.VMEM(base.shape, jnp.float32),
            pltpu.SemaphoreType.DMA((levels,)),
        ],
        compiler_params=PARAMS,
    )(*arguments)


def stage_kernel(plan, count, *refs):
    outs, sems = refs[count:-1], refs[-1]
    copies = []
    for which, place, rows, out, at in plan:
        target = outs[out] if at is None else outs[out].at[pl.ds(at, len(rows) if rows else place)]
        for offset, row in enumerate(rows or (None,)):
            source = refs[which] if row is None else refs[which].at[row]
            if row is not None:
                target = outs[out].at[at + offset]
            copies.append(pltpu.make_async_copy(source, target, sems.at[len(copies)]))
    for copy in copies:
        copy.start()
    for copy in copies:
        copy.wait()


def staged(*items):
    arrays, shapes, specs, plan, copies = [], [], [], [], 0
    for out, (space, parts, rows) in enumerate(items):
        at = 0
        for part in parts:
            size = part.shape[0]
            whole = rows is None and len(parts) == 1
            plan.append((len(arrays), size, rows, out, None if whole else at))
            arrays.append(in_hbm(part) if part.ndim == 3 or space is pltpu.VMEM else part)
            copies += len(rows) if rows else 1
            at += len(rows) if rows else size
        shapes.append(space((at,) + parts[0].shape[1:], parts[0].dtype))
        specs.append(VMEM if space is pltpu.VMEM else SMEM)
    moved = sum(shape.size if hasattr(shape, "size") else 0 for shape in shapes)
    return pl.pallas_call(
        functools.partial(stage_kernel, tuple(plan), len(arrays)),
        out_shape=shapes,
        in_specs=[HBM] * len(arrays),
        out_specs=specs,
        scratch_shapes=[pltpu.SemaphoreType.DMA((copies,))],
        compiler_params=PARAMS,
        cost_estimate=pl.CostEstimate(
            flops=0, bytes_accessed=max(2 * moved, 4_000_000), transcendentals=0
        ),
    )(*arrays)


def pick_kernel(plan, side, me, table, own, *refs):
    sent, out = refs if len(refs) == 2 else (None, refs[0])
    for at, (peer, p) in enumerate(plan):
        for j in range(2):
            for n in range(4):
                local = table[peer, 2 * side + j, n, p] & DUO_BLOCKS - 1
                slot = 4 * j + n
                if sent is None:
                    out[8 * at + slot] = own[(local >> 2 << 1) | (local & 1)]
                else:
                    out[8 * at + slot] = mixed(own, sent, local, me[CORE], 8 + slot)


def pick(me, table, plan, side, own, *sent):
    return pl.pallas_call(
        functools.partial(pick_kernel, tuple(plan), side),
        out_shape=jax.ShapeDtypeStruct((8 * len(plan),) + own.shape[1:], jnp.bfloat16),
        in_specs=[SMEM, SMEM, VMEM] + [VMEM] * len(sent),
        out_specs=VMEM,
        compiler_params=PARAMS,
        cost_estimate=pl.CostEstimate(
            flops=0, bytes_accessed=131072 * len(plan), transcendentals=0
        ),
    )(in_smem(me), in_smem(table), own, *sent)


def halves(p, start=NONE):
    return ("halves", p, start)


def on_device(
    right_sides, lower_inv, upper_inv, lower_off, upper_off, lower_pattern, upper_pattern
):
    sub, group = lax.axis_index("sub"), lax.axis_index("group")
    square, plane, duo = (2, 4, 8), (2, 4, 8, 16), (2, 4, 8, 16, 32)

    tables = [x.transpose(1, 2, 0) for x in (lower_pattern, upper_pattern)]
    f5, sent, mine = first_update(right_sides, lower_inv, *tables, 8)
    across = swapped(mine, "group", 2)
    right, lower_inv, off_first, table, me = staged(
        (pltpu.VMEM, [after(right_sides, sent)], None),
        (pltpu.VMEM, [lower_inv], None),
        (pltpu.VMEM, [lower_off], FIRST),
        (pltpu.SMEM, tables, None),
        (pltpu.SMEM, [positions(sub, group)], None),
    )
    near5, across, me = lax.optimization_barrier((spread(sent, (1, 2, 4)), across, me))
    near5 = (near5,)
    low = functools.partial(update, me, table, off_first, side=0, kept=FIRST)

    f4, sent = low(right, 4, [("one", 14, NONE)], [near5], level=4, inverse=[lower_inv], ways=8)
    near4 = collected(sent, square)
    mates = swapped(after(jnp.stack([mine, across]), near4[0]), "sub", 1)
    (r3,) = low(
        after(right, near4[0]), 3, [("one", 13, NONE)], [near5], level=3, inverse=[lower_inv]
    )
    off_low = premultiplied(after(off_first, near4[0]), FIRST, [(9, 3), (5, 2)], [lower_inv])
    last_low = functools.partial(update, me, table, off_low, side=0, kept=(9, 5))
    near4 = (near4[0], after(near4[1], mates, off_low))
    f3, sent = last_low(r3, None, [halves(9)], [near4], ways=16)
    near3 = collected(sent, plane)
    (peers,) = staged((pltpu.SMEM, [after(across[None], near3[0]), mates], None))
    (r2,) = low(
        after(right, near3[0]),
        2,
        [("one", 12, NONE), halves(8)],
        [near5, near4],
        level=2,
        inverse=[lower_inv],
    )
    near3 = (near3[0], after(near3[1], peers))
    f2, sent = last_low(r2, None, [halves(5)], [near3], ways=32)
    own2 = spread(sent, duo)
    near2 = (own2, swapped(pick(me, peers, [(MATE, 2), (MATE, 1)], 0, own2), "sub", 1))
    (r1,) = low(
        after(right, own2),
        1,
        [("one", 11, NONE), halves(7), halves(4)],
        [near5, near4, near3],
        level=1,
        inverse=[lower_inv],
    )
    off_low = premultiplied(after(off_first, own2), FIRST, [(2, 1)], [lower_inv])
    f1, sent = update(
        me, table, off_low, r1, None, [("core", 2, 0)], [near2], 0, ways=32, kept=(2,)
    )
    own1 = spread(sent, duo)
    near1 = (own1, swapped(pick(me, peers, [(MATE, 0), (MATE_ACROSS, 0)], 0, own1), "sub", 1))
    sent = pick(me, peers, [(ACROSS, 0)], 0, *near1)
    far = swapped(sent, "group", 2)
    lower_off, upper_inv = staged(
        (pltpu.VMEM, [after(lower_off, sent)], None),
        (pltpu.VMEM, [upper_inv], None),
    )
    low = functools.partial(update, me, table, lower_off, side=0)
    (r0,) = low(
        right,
        0,
        [("one", 10, NONE), halves(6), halves(3), ("core", 1, 8)],
        [near5, near4, near3, near2],
        level=0,
        inverse=[lower_inv, upper_inv],
    )
    off_low = premultiplied(lower_off, None, [(0, 0)], [lower_inv, upper_inv])
    far, r0, off_low = lax.optimization_barrier((far, r0, off_low))
    s0, sent = update(
        me, table, off_low, r0, None, [("far", 0, 0)], [near1 + (far,)], 0, ways=32, kept=(0,)
    )

    own0 = spread(sent, duo)
    near0 = (own0, swapped(pick(me, peers, [(MATE, 0), (MATE_ACROSS, 0)], 1, own0), "sub", 1))
    sent = pick(me, peers, [(ACROSS, 0)], 1, *near0)
    far = swapped(sent, "group", 2)
    (upper_off,) = staged((pltpu.VMEM, [after(upper_off, sent)], None))
    other0 = swapped(after(own0, sent), "sub", 1)
    up = functools.partial(update, me, table, upper_off, side=1)
    (r1,) = up(f1, None, [], [], level=1, inverse=[upper_inv])
    entries = [(0, 1), (2, 2), (5, 3), (9, 4), (13, 5), (14, 5)]
    off_up = premultiplied(upper_off, None, entries, [upper_inv])
    kept = tuple(p for p, _ in entries)
    last_up = functools.partial(update, me, table, off_up, side=1, kept=kept)
    far, off_up, other0, r1 = lax.optimization_barrier((far, off_up, other0, r1))
    s1, sent = last_up(r1, None, [("far", 0, 0)], [near0 + (far,)], ways=32)
    near0 = (own0, other0)
    own1 = spread(sent, duo)
    near1 = (own1, swapped(pick(me, peers, [(MATE, 2)], 1, own1), "sub", 1))
    (r2,) = up(after(f2, own1), None, [halves(1)], [near0], level=2, inverse=[upper_inv])
    s2, sent = last_up(r2, None, [("core", 2, 0)], [near1], ways=16)
    near1 = (own1, swapped(after(own1, r2), "sub", 1))
    near2 = collected(sent, plane)
    (r3,) = up(
        after(f3, near2[0]),
        None,
        [halves(3, PLANE64), halves(4, PLANE64)],
        [near0, near1],
        level=3,
        inverse=[upper_inv],
    )
    s3, sent = last_up(r3, None, [halves(5)], [near2], ways=8)
    near3 = collected(sent, square)
    (r4,) = up(
        after(f4, near3[0]),
        None,
        [halves(6, SIXTEEN64), halves(7, SIXTEEN64), halves(8, SIXTEEN32)],
        [near0, near1, near2],
        level=4,
        inverse=[upper_inv],
    )
    (r5,) = up(
        after(f5, near3[0]),
        None,
        [halves(10, EIGHT64), halves(11, EIGHT64), halves(12, EIGHT32)],
        [near0, near1, near2],
        level=5,
        inverse=[upper_inv],
    )
    near3 = (near3[0], after(near3[1], r5))
    s4, sent = last_up(r4, None, [halves(9)], [near3], ways=8)
    near4 = (spread(sent, (1, 2, 4)),)
    return last_update(
        me,
        table,
        off_up,
        r5,
        [halves(13, EIGHT16), ("one", 14, NONE)],
        [near3, near4],
        kept,
        [s0, s1, s2, s3, s4],
    )


def solution(mesh):
    return jax.shard_map(
        on_device,
        mesh=mesh,
        in_specs=(
            P(None, ("group", "sub"), None, None),
            P(None, ("group", "sub"), None, None),
            P(None, ("group", "sub"), None, None),
            P(None, ("group", "sub"), None, None, None),
            P(None, ("group", "sub"), None, None, None),
            P(None, ("group", "sub"), None),
            P(None, ("group", "sub"), None),
        ),
        out_specs=P(None, ("group", "sub"), None, None),
        check_vma=False,
    )
```

```python
import functools

import jax
import jax.numpy as jnp
from jax import lax
from jax.experimental import pallas as pl
from jax.experimental.pallas import tpu as pltpu
from jax.sharding import PartitionSpec as P

DUO_BITS = 7
DUO_BLOCKS = 1 << DUO_BITS
VMEM = pl.BlockSpec(memory_space=pltpu.VMEM)
SMEM = pl.BlockSpec(memory_space=pltpu.SMEM)
HBM = pl.BlockSpec(memory_space=pl.ANY)
PARAMS = pltpu.CompilerParams(vmem_limit_bytes=8 * 2**20)


def span(masks, count):
    groups, seen = [], set()
    for first in range(count):
        if first not in seen:
            group = [first]
            for mask in masks:
                group = group + [member ^ mask for member in group]
            seen.update(group)
            groups.append(sorted(group))
    return groups


def swapped(block, axis, mask):
    return lax.ppermute(block, axis, [(i, i ^ mask) for i in range(lax.axis_size(axis))])


def spread(copies, masks):
    axes = ("group", "sub")
    groups = span(masks, lax.axis_size("group") * lax.axis_size("sub"))
    return lax.all_to_all(copies, axes, 0, 0, tiled=True, axis_index_groups=groups)


def collected(copies, masks):
    own = spread(copies, masks)
    return own, swapped(own, "sub", 1)


def after(value, *others):
    return lax.optimization_barrier((value,) + others)[0]


def in_vmem(value):
    return pltpu.with_memory_space_constraint(value, pltpu.VMEM)


def in_smem(value):
    return pltpu.with_memory_space_constraint(value, pltpu.SMEM)


def in_hbm(value):
    return pltpu.with_memory_space_constraint(value, pltpu.HBM)


(CORE, DUO, PLANE64, SIXTEEN64, EIGHT64, SIXTEEN32, EIGHT32, EIGHT16, NONE) = range(9)
ACROSS, MATE, MATE_ACROSS = range(3)


def positions(sub, group):
    sixteen, eight = (sub >> 4) * 32, (sub >> 3) * 16
    plane = (group & 1) * 64
    return jnp.stack(
        [
            sub & 1,
            (group >> 1) & 1,
            plane,
            plane + sixteen,
            plane + eight,
            sixteen,
            eight,
            (sub >> 3 & 1) * 16,
        ]
    )


def half_of(value, me):
    half = value.shape[0] // 2
    return jnp.where(me[CORE] == 0, value[:half], value[half:])


def read(kind, start, refs, me, wanted, slot):
    local = wanted if start == NONE else wanted + me[start]
    if kind == "one":
        return refs[0][local]
    if kind == "halves":
        index = (local >> 2 << 1) | (local & 1)
        own = (local >> 1 & 1) == me[CORE]
        return jnp.where(own, refs[0][index], refs[1][index])
    if kind == "cols":
        return refs[0][at_chip(local, me)]
    near = refs[0][at_chip(local & DUO_BLOCKS - 1, me)]
    return jnp.where(wanted >> DUO_BITS == me[DUO], near, refs[1][slot])


def at_chip(local, me):
    return local ^ (me[CORE] << 1)


def send(ref, totals):
    values = [total.astype(jnp.bfloat16) for total in totals]
    for way in range(ref.shape[0] // 2):
        for j in range(2):
            ref[2 * way + j] = values[j]


FIRST = (13, 9, 12, 8, 5, 11, 7, 4, 2)
BUFFERS = {"one": 1, "halves": 2, "cols": 1, "far": 2}


def coupled(total, j, plan, near, side, kept, me, table, off):
    for (kind, p, start), buffers in zip(plan, near):
        at = kept.index(p) if kept else p
        picked = [
            read(kind, start, buffers, me, table[2 * side + j, n, p], j * 4 + n) for n in range(4)
        ]
        total = total - jnp.dot(
            jnp.concatenate(picked, 1),
            off[at, j].reshape(512, 128),
            preferred_element_type=jnp.float32,
        )
    return total


def times(total, matrix):
    return jnp.dot(total.astype(jnp.bfloat16), matrix, preferred_element_type=jnp.float32)


def update_kernel(plan, side, kept, first, level, inverses, ways, me, table, off, base, *refs):
    refs = list(refs)
    near = [[refs.pop(0) for _ in range(BUFFERS[entry[0]])] for entry in plan]
    inverse = [refs.pop(0) for _ in range(inverses)]
    totals = [
        coupled(base[first, j] if first is not None else base[j], j, plan, near, side, kept, me, table, off)
        for j in range(2)
    ]
    for matrix in inverse:
        totals = [times(totals[j], matrix[level, j]) for j in range(2)]
    for j in range(2):
        refs[0][j] = totals[j]
    if ways:
        send(refs[-1], totals)


def update(me, table, off, base, first, plan, near, side, level=0, inverse=(), ways=0, kept=None):
    shape = (2,) + base.shape[-2:]
    shapes = [jax.ShapeDtypeStruct(shape, jnp.float32)]
    if ways:
        shapes.append(jax.ShapeDtypeStruct((2 * ways,) + shape[1:], jnp.bfloat16))
    arguments = [in_smem(me), in_smem(table), in_vmem(off), in_vmem(base)]
    for buffers in near:
        arguments += list(buffers)
    arguments += [in_vmem(matrix) for matrix in inverse]
    products = 2 * (4 * len(plan) + len(inverse))
    return pl.pallas_call(
        functools.partial(
            update_kernel, tuple(plan), side, kept, first, level, len(inverse), ways
        ),
        out_shape=shapes,
        in_specs=[SMEM, SMEM] + [VMEM] * (len(arguments) - 2),
        out_specs=[VMEM] * len(shapes),
        compiler_params=PARAMS,
        cost_estimate=pl.CostEstimate(
            flops=products * 2 * 32 * 128 * 128, bytes_accessed=products * 32768, transcendentals=0
        ),
    )(*arguments)


def solve_kernel(plan, side, kept, first, level, inverses, ways, me, table, peers, *refs):
    refs = list(refs)
    off = (refs.pop(0), refs.pop(0))
    base = [refs.pop(0) for _ in range(2 if first is not None else 1)]
    near = [[refs.pop(0) for _ in range(BUFFERS[entry[0]])] for entry in plan]
    inverse = [(refs.pop(0), refs.pop(0)) for _ in range(inverses)]
    totals = []
    for row in range(4):
        whose, j = divmod(row, 2)
        if first is None:
            total = base[0][row]
        else:
            whole = base[whose][first, j] if len(base[whose].shape) == 4 else base[whose][j]
            total = half_of(whole, me)
        for (kind, p, start), buffers in zip(plan, near):
            at = kept.index(p) if kept else p
            picked = []
            for n in range(4):
                place = (2 * side + j, n, p)
                wanted = table[place] if whose == 0 else peers[(MATE,) + place]
                value = read(kind, start, buffers, me, wanted, 4 * row + n)
                picked.append(half_of(value, me) if kind in ("one", "halves") else value)
            total = total - jnp.dot(
                jnp.concatenate(picked, 1),
                off[whose][at, j].reshape(512, 128),
                preferred_element_type=jnp.float32,
            )
        totals.append(total)
    for matrices in inverse:
        totals = [times(totals[row], matrices[row // 2][level, row % 2]) for row in range(4)]
    for row in range(4):
        refs[0][row] = totals[row]
    if ways:
        values = [total.astype(jnp.bfloat16) for total in totals]
        for way in range(ways):
            for row in range(4):
                refs[1][4 * way + row] = values[row]


def solve(me, table, peers, off, base, first, plan, near, side, level=0, inverse=(), ways=0, kept=None):
    bases = list(base) if first is not None else [base]
    rows = bases[0].shape[-2] // 2 if first is not None else base.shape[-2]
    shape = (4, rows, bases[0].shape[-1])
    shapes = [jax.ShapeDtypeStruct(shape, jnp.float32)]
    if ways:
        shapes.append(jax.ShapeDtypeStruct((4 * ways,) + shape[1:], jnp.bfloat16))
    arguments = [in_vmem(array) for array in list(off) + bases]
    for buffers in near:
        arguments += list(buffers)
    for matrices in inverse:
        arguments += [in_vmem(matrix) for matrix in matrices]
    products = 4 * (4 * len(plan) + len(inverse))
    return pl.pallas_call(
        functools.partial(
            solve_kernel, tuple(plan), side, kept, first, level, len(inverse), ways
        ),
        out_shape=shapes,
        in_specs=[SMEM] * 3 + [VMEM] * len(arguments),
        out_specs=[VMEM] * len(shapes),
        compiler_params=PARAMS,
        cost_estimate=pl.CostEstimate(
            flops=products * 2 * 16 * 128 * 128, bytes_accessed=products * 32768, transcendentals=0
        ),
    )(in_smem(me), in_smem(table), in_smem(peers), *arguments)


def first_kernel(level, base, matrix, lower, upper, out, low, joined, right, inverse, sems):
    rows = lower.shape[0]
    copies = [
        pltpu.make_async_copy(base.at[level], right, sems.at[0]),
        pltpu.make_async_copy(matrix.at[level], inverse, sems.at[1]),
        pltpu.make_async_copy(lower, joined.at[pl.ds(0, rows)], sems.at[2]),
        pltpu.make_async_copy(upper, joined.at[pl.ds(rows, rows)], sems.at[3]),
    ]
    for copy in copies:
        copy.start()
    copies[0].wait()
    copies[1].wait()
    totals = [times(right[j], inverse[j]) for j in range(2)]
    for j in range(2):
        out[j] = totals[j]
    send(low, totals)
    copies[2].wait()
    copies[3].wait()


def first_update(right_sides, inverse, lower, upper, ways):
    levels = right_sides.shape[0]
    shape, matrix = right_sides.shape[1:], inverse.shape[1:]
    return pl.pallas_call(
        functools.partial(first_kernel, levels - 1),
        out_shape=[
            jax.ShapeDtypeStruct(shape, jnp.float32),
            jax.ShapeDtypeStruct((2 * ways,) + shape[1:], jnp.bfloat16),
            jax.ShapeDtypeStruct((2 * lower.shape[0],) + lower.shape[1:], lower.dtype),
        ],
        in_specs=[HBM] * 4,
        out_specs=[VMEM] * 3,
        scratch_shapes=[
            pltpu.VMEM(shape, jnp.float32),
            pltpu.VMEM(matrix, jnp.bfloat16),
            pltpu.SemaphoreType.DMA((4,)),
        ],
        compiler_params=PARAMS,
    )(in_hbm(right_sides), in_hbm(inverse), in_hbm(lower), in_hbm(upper))


def pack_kernel(*refs):
    for level, ref in enumerate(refs[:-1]):
        refs[-1][level] = ref[2:]


def pack(solved):
    shape = solved[0].shape
    return pl.pallas_call(
        pack_kernel,
        out_shape=jax.ShapeDtypeStruct((len(solved), shape[0] - 2) + shape[1:], jnp.float32),
        in_specs=[VMEM] * len(solved),
        out_specs=VMEM,
        compiler_params=PARAMS,
    )(*[in_vmem(value) for value in solved])


def last_kernel(me, sent, *refs):
    out, sems = refs[-2:]
    half = sent.shape[-2]
    mine = pl.ds(pl.multiple_of(me[CORE] * half, half), half)
    other = pl.ds(pl.multiple_of((1 - me[CORE]) * half, half), half)
    copies = []
    for level, ref in enumerate(refs[:-2]):
        for j in range(2):
            for source, cols in ((ref.at[j], mine), (sent.at[level, j], other)):
                target = out.at[level, j, cols]
                copies.append(pltpu.make_async_copy(source, target, sems.at[len(copies)]))
    for copy in copies:
        copy.start()
    for copy in copies:
        copy.wait()


def last_update(me, sent, solved):
    levels, rows, half, width = sent.shape
    return pl.pallas_call(
        last_kernel,
        out_shape=jax.ShapeDtypeStruct((levels, rows, 2 * half, width), jnp.float32),
        in_specs=[SMEM] + [VMEM] * (1 + levels),
        out_specs=HBM,
        scratch_shapes=[pltpu.SemaphoreType.DMA((4 * levels,))],
        compiler_params=PARAMS,
    )(in_smem(me), in_vmem(sent), *[in_vmem(value) for value in solved])


def stage_kernel(plan, count, *refs):
    outs, sems = refs[count:-1], refs[-1]
    copies = []
    for which, place, rows, out, at in plan:
        target = outs[out] if at is None else outs[out].at[pl.ds(at, len(rows) if rows else place)]
        for offset, row in enumerate(rows or (None,)):
            source = refs[which] if row is None else refs[which].at[row]
            if row is not None:
                target = outs[out].at[at + offset]
            copies.append(pltpu.make_async_copy(source, target, sems.at[len(copies)]))
    for copy in copies:
        copy.start()
    for copy in copies:
        copy.wait()


def staged(*items):
    arrays, shapes, specs, plan, copies = [], [], [], [], 0
    for out, (space, parts, rows) in enumerate(items):
        at = 0
        for part in parts:
            size = part.shape[0]
            whole = rows is None and len(parts) == 1
            plan.append((len(arrays), size, rows, out, None if whole else at))
            arrays.append(in_hbm(part) if part.ndim == 3 or space is pltpu.VMEM else part)
            copies += len(rows) if rows else 1
            at += len(rows) if rows else size
        shapes.append(space((at,) + parts[0].shape[1:], parts[0].dtype))
        specs.append(VMEM if space is pltpu.VMEM else SMEM)
    moved = sum(shape.size if hasattr(shape, "size") else 0 for shape in shapes)
    return pl.pallas_call(
        functools.partial(stage_kernel, tuple(plan), len(arrays)),
        out_shape=shapes,
        in_specs=[HBM] * len(arrays),
        out_specs=specs,
        scratch_shapes=[pltpu.SemaphoreType.DMA((copies,))],
        compiler_params=PARAMS,
        cost_estimate=pl.CostEstimate(
            flops=0, bytes_accessed=max(2 * moved, 4_000_000), transcendentals=0
        ),
    )(*arrays)


def pick_kernel(side, me, peers, near, out):
    for row in range(4):
        whose, j = divmod(row, 2)
        peer = (ACROSS, MATE_ACROSS)[whose]
        for n in range(4):
            local = peers[peer, 2 * side + j, n, 0] & DUO_BLOCKS - 1
            out[4 * row + n] = near[at_chip(local, me)]


def pick(me, peers, side, near):
    return pl.pallas_call(
        functools.partial(pick_kernel, side),
        out_shape=jax.ShapeDtypeStruct((16,) + near.shape[1:], jnp.bfloat16),
        in_specs=[SMEM, SMEM, VMEM],
        out_specs=VMEM,
        compiler_params=PARAMS,
        cost_estimate=pl.CostEstimate(flops=0, bytes_accessed=131072, transcendentals=0),
    )(in_smem(me), in_smem(peers), near)


def cols(p, start=NONE):
    return ("cols", p, start)


def on_device(
    right_sides, lower_inv, upper_inv, lower_off, upper_off, lower_pattern, upper_pattern
):
    sub, group = lax.axis_index("sub"), lax.axis_index("group")
    square, plane, duo = (2, 4, 8), (2, 4, 8, 16), (2, 4, 8, 16, 32)

    tables = [x.transpose(1, 2, 0) for x in (lower_pattern, upper_pattern)]
    f5, sent, mine = first_update(right_sides, lower_inv, *tables, 8)
    across = swapped(mine, "group", 2)
    lower_all, inverse_all = after(lower_off, sent), lower_inv
    right, lower_inv, off14, off_first, table, me = staged(
        (pltpu.VMEM, [after(right_sides, sent)], None),
        (pltpu.VMEM, [lower_inv], None),
        (pltpu.VMEM, [lower_off], (14,)),
        (pltpu.VMEM, [lower_off], FIRST),
        (pltpu.SMEM, tables, None),
        (pltpu.SMEM, [positions(sub, group)], None),
    )
    near5, across, me = lax.optimization_barrier((spread(sent, (1, 2, 4)), across, me))
    f4, sent = update(
        me, table, off14, right, 4, [("one", 14, NONE)], [(near5,)], 0, 4, [lower_inv], 8, (14,)
    )
    theirs = [swapped(x, "sub", 1) for x in (right_sides, lower_all, inverse_all, upper_inv)]
    near4, *theirs = lax.optimization_barrier((spread(sent, square), *theirs))
    near4 = (near4, swapped(near4, "sub", 1))
    mates = swapped(after(jnp.stack([mine, across]), near4[0]), "sub", 1)
    f4_mate = swapped(after(f4, near4[0]), "sub", 1)
    f5_mate = swapped(after(f5, near4[0]), "sub", 1)
    peers, right_mate, inv_mate, off_mate = staged(
        (pltpu.SMEM, [across[None], mates], None),
        (pltpu.VMEM, [theirs[0]], None),
        (pltpu.VMEM, [theirs[2]], None),
        (pltpu.VMEM, [theirs[1]], FIRST),
    )
    near4 = (near4[0], after(near4[1], right_mate, f4_mate, f5_mate))

    low = functools.partial(
        solve, me, table, peers, (off_first, off_mate), side=0, kept=FIRST, inverse=[(lower_inv, inv_mate)]
    )
    right = (right, right_mate)
    f3, sent = low(
        right, 3, [("one", 13, NONE), ("halves", 9, NONE)], [(near5,), near4], level=3, ways=16
    )
    near3 = (spread(sent, plane),)
    f2, sent = low(
        right,
        2,
        [("one", 12, NONE), ("halves", 8, NONE), cols(5)],
        [(near5,), near4, near3],
        level=2,
        ways=32,
    )
    near2 = (spread(sent, duo),)
    f1, sent = low(
        right,
        1,
        [("one", 11, NONE), ("halves", 7, NONE), cols(4), cols(2)],
        [(near5,), near4, near3, near2],
        level=1,
        ways=32,
    )
    near1 = spread(sent, duo)
    sent = pick(me, peers, 0, near1)
    far = swapped(sent, "group", 2)
    lower_off, low_mate, upper_inv, up_inv_mate = staged(
        (pltpu.VMEM, [after(lower_off, sent)], None),
        (pltpu.VMEM, [theirs[1]], None),
        (pltpu.VMEM, [upper_inv], None),
        (pltpu.VMEM, [theirs[3]], None),
    )
    low = functools.partial(solve, me, table, peers, (lower_off, low_mate), side=0)
    (r0,) = low(
        right,
        0,
        [("one", 10, NONE), ("halves", 6, NONE), cols(3), cols(1)],
        [(near5,), near4, near3, near2],
    )
    far, r0 = lax.optimization_barrier((far, r0))
    s0, sent = low(
        r0,
        None,
        [("far", 0, NONE)],
        [(near1, far)],
        level=0,
        inverse=[(lower_inv, inv_mate), (upper_inv, up_inv_mate)],
        ways=32,
    )

    up_mate = swapped(upper_off, "sub", 1)
    near0 = spread(sent, duo)
    sent = pick(me, peers, 1, near0)
    far = swapped(sent, "group", 2)
    upper_off, up_mate = staged(
        (pltpu.VMEM, [after(upper_off, sent)], None), (pltpu.VMEM, [after(up_mate, sent)], None)
    )
    far, upper_off = lax.optimization_barrier((far, upper_off))
    up = functools.partial(
        solve, me, table, peers, (upper_off, up_mate), side=1, inverse=[(upper_inv, up_inv_mate)]
    )
    s1, sent = up(f1, None, [("far", 0, NONE)], [(near0, far)], level=1, ways=32)
    near0, near1 = (near0,), (spread(sent, duo),)
    s2, sent = up(f2, None, [cols(1), cols(2)], [near0, near1], level=2, ways=16)
    near2 = (spread(sent, plane),)
    s3, sent = up(
        f3,
        None,
        [cols(3, PLANE64), cols(4, PLANE64), cols(5)],
        [near0, near1, near2],
        level=3,
        ways=8,
    )
    near3 = (spread(sent, square),)
    s4, sent = up(
        (f4, f4_mate),
        0,
        [cols(6, SIXTEEN64), cols(7, SIXTEEN64), cols(8, SIXTEEN32), cols(9)],
        [near0, near1, near2, near3],
        level=4,
        ways=4,
    )
    near4 = (spread(sent, (2, 4)),)
    (s5,) = up(
        (f5, f5_mate),
        0,
        [cols(10, EIGHT64), cols(11, EIGHT64), cols(12, EIGHT32), cols(13, EIGHT16), cols(14)],
        [near0, near1, near2, near3, near4],
        level=5,
    )
    solved = [s0, s1, s2, s3, s4, s5]
    sent = swapped(pack(solved), "sub", 1)
    return last_update(me, sent, solved)


def solution(mesh):
    return jax.shard_map(
        on_device,
        mesh=mesh,
        in_specs=(
            P(None, ("group", "sub"), None, None),
            P(None, ("group", "sub"), None, None),
            P(None, ("group", "sub"), None, None),
            P(None, ("group", "sub"), None, None, None),
            P(None, ("group", "sub"), None, None, None),
            P(None, ("group", "sub"), None),
            P(None, ("group", "sub"), None),
        ),
        out_specs=P(None, ("group", "sub"), None, None),
        check_vma=False,
    )
```

```python
import functools

import jax
import jax.numpy as jnp
from jax import lax
from jax.experimental import pallas as pl
from jax.experimental.pallas import tpu as pltpu
from jax.sharding import PartitionSpec as P

DUO_BITS = 7
DUO_BLOCKS = 1 << DUO_BITS
VMEM = pl.BlockSpec(memory_space=pltpu.VMEM)
SMEM = pl.BlockSpec(memory_space=pltpu.SMEM)
HBM = pl.BlockSpec(memory_space=pl.ANY)
PARAMS = pltpu.CompilerParams(vmem_limit_bytes=8 * 2**20)


def span(masks, count):
    groups, seen = [], set()
    for first in range(count):
        if first not in seen:
            group = [first]
            for mask in masks:
                group = group + [member ^ mask for member in group]
            seen.update(group)
            groups.append(sorted(group))
    return groups


def swapped(block, axis, mask):
    return lax.ppermute(block, axis, [(i, i ^ mask) for i in range(lax.axis_size(axis))])


def spread(copies, masks):
    axes = ("group", "sub")
    groups = span(masks, lax.axis_size("group") * lax.axis_size("sub"))
    return lax.all_to_all(copies, axes, 0, 0, tiled=True, axis_index_groups=groups)


def collected(copies, masks):
    own = spread(copies, masks)
    return own, swapped(own, "sub", 1)


def after(value, *others):
    return lax.optimization_barrier((value,) + others)[0]


def in_vmem(value):
    return pltpu.with_memory_space_constraint(value, pltpu.VMEM)


def in_smem(value):
    return pltpu.with_memory_space_constraint(value, pltpu.SMEM)


def in_hbm(value):
    return pltpu.with_memory_space_constraint(value, pltpu.HBM)


(CORE, DUO, PLANE64, SIXTEEN64, EIGHT64, SIXTEEN32, EIGHT32, EIGHT16, NONE) = range(9)
ACROSS, MATE_ACROSS, MATE = range(3)


def positions(sub, group):
    sixteen, eight = (sub >> 4) * 32, (sub >> 3) * 16
    plane = (group & 1) * 64
    return jnp.stack(
        [
            sub & 1,
            (group >> 1) & 1,
            plane,
            plane + sixteen,
            plane + eight,
            sixteen,
            eight,
            (sub >> 3 & 1) * 16,
        ]
    )


def half_of(value, me):
    half = value.shape[0] // 2
    return jnp.where(me[CORE] == 0, value[:half], value[half:])


def read(kind, start, refs, me, wanted, slot):
    local = wanted if start == NONE else wanted + me[start]
    if kind == "one":
        return refs[0][local]
    if kind == "halves":
        index = (local >> 2 << 1) | (local & 1)
        own = (local >> 1 & 1) == me[CORE]
        return jnp.where(own, refs[0][index], refs[1][index])
    if kind == "cols":
        return refs[0][at_chip(local, me)]
    near = refs[0][at_chip(local & DUO_BLOCKS - 1, me)]
    return jnp.where(wanted >> DUO_BITS == me[DUO], near, refs[1][slot])


def at_chip(local, me):
    return local ^ (me[CORE] << 1)


def send(ref, totals):
    values = [total.astype(jnp.bfloat16) for total in totals]
    for way in range(ref.shape[0] // 2):
        for j in range(2):
            ref[2 * way + j] = values[j]


FIRST = (13, 9, 12, 8, 5, 11, 7, 4, 2)
LAST = (10, 6, 3, 1, 0)
BUFFERS = {"one": 1, "halves": 2, "cols": 1, "far": 2}


def coupled(total, j, plan, near, side, kept, me, table, off):
    for (kind, p, start), buffers in zip(plan, near):
        at = kept.index(p) if kept else p
        picked = [
            read(kind, start, buffers, me, table[2 * side + j, n, p], j * 4 + n) for n in range(4)
        ]
        total = total - jnp.dot(
            jnp.concatenate(picked, 1),
            off[at, j].reshape(512, 128),
            preferred_element_type=jnp.float32,
        )
    return total


def times(total, matrix):
    return jnp.dot(total.astype(jnp.bfloat16), matrix, preferred_element_type=jnp.float32)


def update_kernel(plan, side, kept, first, level, inverses, ways, me, table, off, base, *refs):
    refs = list(refs)
    near = [[refs.pop(0) for _ in range(BUFFERS[entry[0]])] for entry in plan]
    inverse = [refs.pop(0) for _ in range(inverses)]
    totals = [
        coupled(base[first, j] if first is not None else base[j], j, plan, near, side, kept, me, table, off)
        for j in range(2)
    ]
    for matrix in inverse:
        totals = [times(totals[j], matrix[level, j]) for j in range(2)]
    for j in range(2):
        refs[0][j] = totals[j]
    if ways:
        send(refs[-1], totals)


def update(me, table, off, base, first, plan, near, side, level=0, inverse=(), ways=0, kept=None):
    shape = (2,) + base.shape[-2:]
    shapes = [jax.ShapeDtypeStruct(shape, jnp.float32)]
    if ways:
        shapes.append(jax.ShapeDtypeStruct((2 * ways,) + shape[1:], jnp.bfloat16))
    arguments = [in_smem(me), in_smem(table), in_vmem(off), in_vmem(base)]
    for buffers in near:
        arguments += list(buffers)
    arguments += [in_vmem(matrix) for matrix in inverse]
    products = 2 * (4 * len(plan) + len(inverse))
    return pl.pallas_call(
        functools.partial(
            update_kernel, tuple(plan), side, kept, first, level, len(inverse), ways
        ),
        out_shape=shapes,
        in_specs=[SMEM, SMEM] + [VMEM] * (len(arguments) - 2),
        out_specs=[VMEM] * len(shapes),
        compiler_params=PARAMS,
        cost_estimate=pl.CostEstimate(
            flops=products * 2 * 32 * 128 * 128, bytes_accessed=products * 32768, transcendentals=0
        ),
    )(*arguments)


def solve_kernel(plan, side, kept, first, level, inverses, ways, me, table, peers, *refs):
    refs = list(refs)
    off = (refs.pop(0), refs.pop(0))
    base = [refs.pop(0) for _ in range(2 if first is not None else 1)]
    near = [[refs.pop(0) for _ in range(BUFFERS[entry[0]])] for entry in plan]
    inverse = [(refs.pop(0), refs.pop(0)) for _ in range(inverses)]
    totals = []
    for row in range(4):
        whose, j = divmod(row, 2)
        if first is None:
            total = base[0][row]
        else:
            whole = base[whose][first, j] if len(base[whose].shape) == 4 else base[whose][j]
            total = half_of(whole, me)
        for (kind, p, start), buffers in zip(plan, near):
            at = kept.index(p) if kept else p
            picked = []
            for n in range(4):
                place = (2 * side + j, n, p)
                wanted = table[place] if whose == 0 else peers[(MATE,) + place]
                value = read(kind, start, buffers, me, wanted, 4 * row + n)
                picked.append(half_of(value, me) if kind in ("one", "halves") else value)
            total = total - jnp.dot(
                jnp.concatenate(picked, 1),
                off[whose][at, j].reshape(512, 128),
                preferred_element_type=jnp.float32,
            )
        totals.append(total)
    for matrices in inverse:
        totals = [times(totals[row], matrices[row // 2][level, row % 2]) for row in range(4)]
    for row in range(4):
        refs[0][row] = totals[row]
    if ways:
        values = [total.astype(jnp.bfloat16) for total in totals]
        for way in range(ways):
            for row in range(4):
                refs[1][4 * way + row] = values[row]


def solve(me, table, peers, off, base, first, plan, near, side, level=0, inverse=(), ways=0, kept=None):
    bases = list(base) if first is not None else [base]
    rows = bases[0].shape[-2] // 2 if first is not None else base.shape[-2]
    shape = (4, rows, bases[0].shape[-1])
    shapes = [jax.ShapeDtypeStruct(shape, jnp.float32)]
    if ways:
        shapes.append(jax.ShapeDtypeStruct((4 * ways,) + shape[1:], jnp.bfloat16))
    arguments = [in_vmem(array) for array in list(off) + bases]
    for buffers in near:
        arguments += list(buffers)
    for matrices in inverse:
        arguments += [in_vmem(matrix) for matrix in matrices]
    products = 4 * (4 * len(plan) + len(inverse))
    return pl.pallas_call(
        functools.partial(
            solve_kernel, tuple(plan), side, kept, first, level, len(inverse), ways
        ),
        out_shape=shapes,
        in_specs=[SMEM] * 3 + [VMEM] * len(arguments),
        out_specs=[VMEM] * len(shapes),
        compiler_params=PARAMS,
        cost_estimate=pl.CostEstimate(
            flops=products * 2 * 16 * 128 * 128, bytes_accessed=products * 32768, transcendentals=0
        ),
    )(in_smem(me), in_smem(table), in_smem(peers), *arguments)


def first_kernel(level, base, matrix, lower, upper, out, low, joined, right, inverse, sems):
    rows = lower.shape[0]
    copies = [
        pltpu.make_async_copy(base.at[level], right, sems.at[0]),
        pltpu.make_async_copy(matrix.at[level], inverse, sems.at[1]),
        pltpu.make_async_copy(lower, joined.at[pl.ds(0, rows)], sems.at[2]),
        pltpu.make_async_copy(upper, joined.at[pl.ds(rows, rows)], sems.at[3]),
    ]
    for copy in copies:
        copy.start()
    copies[0].wait()
    copies[1].wait()
    totals = [times(right[j], inverse[j]) for j in range(2)]
    for j in range(2):
        out[j] = totals[j]
    send(low, totals)
    copies[2].wait()
    copies[3].wait()


def first_update(right_sides, inverse, lower, upper, ways):
    levels = right_sides.shape[0]
    shape, matrix = right_sides.shape[1:], inverse.shape[1:]
    return pl.pallas_call(
        functools.partial(first_kernel, levels - 1),
        out_shape=[
            jax.ShapeDtypeStruct(shape, jnp.float32),
            jax.ShapeDtypeStruct((2 * ways,) + shape[1:], jnp.bfloat16),
            jax.ShapeDtypeStruct((2 * lower.shape[0],) + lower.shape[1:], lower.dtype),
        ],
        in_specs=[HBM] * 4,
        out_specs=[VMEM] * 3,
        scratch_shapes=[
            pltpu.VMEM(shape, jnp.float32),
            pltpu.VMEM(matrix, jnp.bfloat16),
            pltpu.SemaphoreType.DMA((4,)),
        ],
        compiler_params=PARAMS,
    )(in_hbm(right_sides), in_hbm(inverse), in_hbm(lower), in_hbm(upper))


def pack_kernel(*refs):
    for level, ref in enumerate(refs[:-1]):
        refs[-1][level] = ref[2:]


def pack(solved):
    shape = solved[0].shape
    return pl.pallas_call(
        pack_kernel,
        out_shape=jax.ShapeDtypeStruct((len(solved), shape[0] - 2) + shape[1:], jnp.float32),
        in_specs=[VMEM] * len(solved),
        out_specs=VMEM,
        compiler_params=PARAMS,
    )(*[in_vmem(value) for value in solved])


def last_kernel(me, sent, *refs):
    out, sems = refs[-2:]
    half = sent.shape[-2]
    mine = pl.ds(pl.multiple_of(me[CORE] * half, half), half)
    other = pl.ds(pl.multiple_of((1 - me[CORE]) * half, half), half)
    copies = []
    for level, ref in enumerate(refs[:-2]):
        for j in range(2):
            for source, cols in ((ref.at[j], mine), (sent.at[level, j], other)):
                target = out.at[level, j, cols]
                copies.append(pltpu.make_async_copy(source, target, sems.at[len(copies)]))
    for copy in copies:
        copy.start()
    for copy in copies:
        copy.wait()


def last_update(me, sent, solved):
    levels, rows, half, width = sent.shape
    return pl.pallas_call(
        last_kernel,
        out_shape=jax.ShapeDtypeStruct((levels, rows, 2 * half, width), jnp.float32),
        in_specs=[SMEM] + [VMEM] * (1 + levels),
        out_specs=HBM,
        scratch_shapes=[pltpu.SemaphoreType.DMA((4 * levels,))],
        compiler_params=PARAMS,
    )(in_smem(me), in_vmem(sent), *[in_vmem(value) for value in solved])


def stage_kernel(plan, count, *refs):
    outs, sems = refs[count:-1], refs[-1]
    copies = []
    for which, place, rows, out, at in plan:
        target = outs[out] if at is None else outs[out].at[pl.ds(at, len(rows) if rows else place)]
        for offset, row in enumerate(rows or (None,)):
            source = refs[which] if row is None else refs[which].at[row]
            if row is not None:
                target = outs[out].at[at + offset]
            copies.append(pltpu.make_async_copy(source, target, sems.at[len(copies)]))
    for copy in copies:
        copy.start()
    for copy in copies:
        copy.wait()


def staged(*items):
    arrays, shapes, specs, plan, copies = [], [], [], [], 0
    for out, (space, parts, rows) in enumerate(items):
        at = 0
        for part in parts:
            size = part.shape[0]
            whole = rows is None and len(parts) == 1
            plan.append((len(arrays), size, rows, out, None if whole else at))
            arrays.append(in_hbm(part) if part.ndim == 3 or space is pltpu.VMEM else part)
            copies += len(rows) if rows else 1
            at += len(rows) if rows else size
        shapes.append(space((at,) + parts[0].shape[1:], parts[0].dtype))
        specs.append(VMEM if space is pltpu.VMEM else SMEM)
    moved = sum(shape.size if hasattr(shape, "size") else 0 for shape in shapes)
    return pl.pallas_call(
        functools.partial(stage_kernel, tuple(plan), len(arrays)),
        out_shape=shapes,
        in_specs=[HBM] * len(arrays),
        out_specs=specs,
        scratch_shapes=[pltpu.SemaphoreType.DMA((copies,))],
        compiler_params=PARAMS,
        cost_estimate=pl.CostEstimate(
            flops=0, bytes_accessed=max(2 * moved, 4_000_000), transcendentals=0
        ),
    )(*arrays)


def pick_kernel(side, me, peers, near, out):
    for row in range(4):
        whose, j = divmod(row, 2)
        peer = (ACROSS, MATE_ACROSS)[whose]
        for n in range(4):
            local = peers[peer, 2 * side + j, n, 0] & DUO_BLOCKS - 1
            out[4 * row + n] = near[at_chip(local, me)]


def pick(me, peers, side, near):
    return pl.pallas_call(
        functools.partial(pick_kernel, side),
        out_shape=jax.ShapeDtypeStruct((16,) + near.shape[1:], jnp.bfloat16),
        in_specs=[SMEM, SMEM, VMEM],
        out_specs=VMEM,
        compiler_params=PARAMS,
        cost_estimate=pl.CostEstimate(flops=0, bytes_accessed=131072, transcendentals=0),
    )(in_smem(me), in_smem(peers), near)


def cols(p, start=NONE):
    return ("cols", p, start)


def on_device(
    right_sides, lower_inv, upper_inv, lower_off, upper_off, lower_pattern, upper_pattern
):
    sub, group = lax.axis_index("sub"), lax.axis_index("group")
    square, plane, duo = (2, 4, 8), (2, 4, 8, 16), (2, 4, 8, 16, 32)

    tables = [x.transpose(1, 2, 0) for x in (lower_pattern, upper_pattern)]
    f5, sent, mine = first_update(right_sides, lower_inv, *tables, 8)
    mate = jnp.concatenate([swapped(x, "sub", 1) for x in tables])
    across = swapped(jnp.stack([mine, mate]), "group", 2)
    lower_all, inverse_all = lower_off, lower_inv
    right, lower_inv, off14, off_first, table, me = staged(
        (pltpu.VMEM, [after(right_sides, sent)], None),
        (pltpu.VMEM, [lower_inv], None),
        (pltpu.VMEM, [lower_off], (14,)),
        (pltpu.VMEM, [lower_off], FIRST),
        (pltpu.SMEM, tables, None),
        (pltpu.SMEM, [positions(sub, group)], None),
    )
    near5, across, me = lax.optimization_barrier((spread(sent, (1, 2, 4)), across, me))
    f4, sent = update(
        me, table, off14, right, 4, [("one", 14, NONE)], [(near5,)], 0, 4, [lower_inv], 8, (14,)
    )
    theirs = [right_sides, lower_all, inverse_all, upper_inv]
    theirs = [swapped(after(x, across), "sub", 1) for x in theirs]
    (peers,) = staged((pltpu.SMEM, [across, mate[None]], None))
    near4, peers, *theirs = lax.optimization_barrier((spread(sent, square), peers, *theirs))
    near4 = (near4, swapped(near4, "sub", 1))
    f4_mate = swapped(after(f4, near4[0]), "sub", 1)
    f5_mate = swapped(after(f5, near4[0]), "sub", 1)
    right_mate, inv_mate, off_mate = staged(
        (pltpu.VMEM, [theirs[0]], None),
        (pltpu.VMEM, [theirs[2]], None),
        (pltpu.VMEM, [theirs[1]], FIRST),
    )
    near4 = (near4[0], after(near4[1], right_mate, f4_mate, f5_mate))

    low = functools.partial(
        solve, me, table, peers, (off_first, off_mate), side=0, kept=FIRST, inverse=[(lower_inv, inv_mate)]
    )
    right = (right, right_mate)
    f3, sent = low(
        right, 3, [("one", 13, NONE), ("halves", 9, NONE)], [(near5,), near4], level=3, ways=16
    )
    near3 = (spread(sent, plane),)
    f2, sent = low(
        right,
        2,
        [("one", 12, NONE), ("halves", 8, NONE), cols(5)],
        [(near5,), near4, near3],
        level=2,
        ways=32,
    )
    near2 = (spread(sent, duo),)
    f1, sent = low(
        right,
        1,
        [("one", 11, NONE), ("halves", 7, NONE), cols(4), cols(2)],
        [(near5,), near4, near3, near2],
        level=1,
        ways=32,
    )
    near1 = spread(sent, duo)
    sent = pick(me, peers, 0, near1)
    far = swapped(sent, "group", 2)
    lower_off, low_mate, upper_inv, up_inv_mate = staged(
        (pltpu.VMEM, [after(lower_off, sent)], LAST),
        (pltpu.VMEM, [theirs[1]], LAST),
        (pltpu.VMEM, [upper_inv], None),
        (pltpu.VMEM, [theirs[3]], None),
    )
    low = functools.partial(solve, me, table, peers, (lower_off, low_mate), side=0, kept=LAST)
    (r0,) = low(
        right,
        0,
        [("one", 10, NONE), ("halves", 6, NONE), cols(3), cols(1)],
        [(near5,), near4, near3, near2],
    )
    far, r0 = lax.optimization_barrier((far, r0))
    s0, sent = low(
        r0,
        None,
        [("far", 0, NONE)],
        [(near1, far)],
        level=0,
        inverse=[(lower_inv, inv_mate), (upper_inv, up_inv_mate)],
        ways=32,
    )

    up_mate = swapped(upper_off, "sub", 1)
    near0 = spread(sent, duo)
    sent = pick(me, peers, 1, near0)
    far = swapped(sent, "group", 2)
    upper_off, up_mate = staged(
        (pltpu.VMEM, [after(upper_off, sent)], None), (pltpu.VMEM, [after(up_mate, sent)], None)
    )
    far, upper_off = lax.optimization_barrier((far, upper_off))
    up = functools.partial(
        solve, me, table, peers, (upper_off, up_mate), side=1, inverse=[(upper_inv, up_inv_mate)]
    )
    s1, sent = up(f1, None, [("far", 0, NONE)], [(near0, far)], level=1, ways=32)
    near0, near1 = (near0,), (spread(sent, duo),)
    s2, sent = up(f2, None, [cols(1), cols(2)], [near0, near1], level=2, ways=16)
    near2 = (spread(sent, plane),)
    s3, sent = up(
        f3,
        None,
        [cols(3, PLANE64), cols(4, PLANE64), cols(5)],
        [near0, near1, near2],
        level=3,
        ways=8,
    )
    near3 = (spread(sent, square),)
    s4, sent = up(
        (f4, f4_mate),
        0,
        [cols(6, SIXTEEN64), cols(7, SIXTEEN64), cols(8, SIXTEEN32), cols(9)],
        [near0, near1, near2, near3],
        level=4,
        ways=4,
    )
    near4 = (spread(sent, (2, 4)),)
    (s5,) = up(
        (f5, f5_mate),
        0,
        [cols(10, EIGHT64), cols(11, EIGHT64), cols(12, EIGHT32), cols(13, EIGHT16), cols(14)],
        [near0, near1, near2, near3, near4],
        level=5,
    )
    solved = [s0, s1, s2, s3, s4, s5]
    sent = swapped(pack(solved), "sub", 1)
    return last_update(me, sent, solved)


def solution(mesh):
    return jax.shard_map(
        on_device,
        mesh=mesh,
        in_specs=(
            P(None, ("group", "sub"), None, None),
            P(None, ("group", "sub"), None, None),
            P(None, ("group", "sub"), None, None),
            P(None, ("group", "sub"), None, None, None),
            P(None, ("group", "sub"), None, None, None),
            P(None, ("group", "sub"), None),
            P(None, ("group", "sub"), None),
        ),
        out_specs=P(None, ("group", "sub"), None, None),
        check_vma=False,
    )
```
